128 devices in a mesh: table: 64 (over z, y, x_hi, core), row: 2 (over x_lo).
Axes of the slice: x: 4 (x_hi: 2, x_lo: 2; x = x_hi * 2 + x_lo), y: 4, z: 4, core: 2. Of those that a mesh axis runs over, the one named last changes fastest.
Arguments:
- ids: int32 [4096, 512, 8], P(None, 'table'), may hold values from 0 to 511
- lengths: int32 [4096, 512], P(None, 'table'), may hold values from 1 to 8
- tables: bfloat16 [512, 512, 128], P('table', 'row'), may hold values from -5 to 5
- cross_down: bfloat16 [65536, 256], P('row'), may hold values from -0.0234375 to 0.0234375
- cross_up: bfloat16 [256, 65536], P(None, 'row'), may hold values from -0.375 to 0.375
- bias: float32 [65536], P('row'), may hold values from -4 to 4
- grad_out: bfloat16 [4096, 65536], P('table', 'row'), may hold values from -4 to 4
Outputs:
- crossed: bfloat16 [4096, 65536], P('table', 'row')
- table_grad: bfloat16 [512, 512, 128], P('table', 'row')
The draws below stay inside these ranges and needn't reach their ends.
Inputs may be any that keep to these rules, and one draw needn't show every extreme that they name: ids index the rows of the feature's own table.
All inputs are finite; a program needn't handle non-finite values.
Results may differ from the reference program's by a relative error of at most 0.0061.
Values may be sent and summed in bfloat16 or wider, within the bound.
No kernel may reach another device: no remote copies, remote signals or barrier semaphores. Data moves between devices by JAX's collectives and lax.ppermute only.
A program may use at most 256 MiB of HBM per device.

```python
import math
import jax
import jax.numpy as jnp
import numpy as np
from jax import lax

F = 512
E = 128
R = 256
BAG = 8
BATCH = 4096
VOCAB = 512
PAIR = 4
FE = 65536
N_TABLE = 64
N_ROW = 2


def with_ends(drawn, stream_key, least, high):
    longest = drawn.shape.index(max(drawn.shape))
    spots = []
    for shift in (0, 1):
        where = [jax.random.randint(jax.random.fold_in(stream_key, axis), (), 0, length) for axis, length in enumerate(drawn.shape)]
        where[longest] = (where[longest] + shift) % drawn.shape[longest]
        spots.append(tuple(where))
    return drawn.at[spots[0]].set(least).at[spots[1]].set(high)


def steps_of(key, shape, shards, smallest, top_value):
    def one(dim, blocks):
        draws = jax.random.uniform(jax.random.fold_in(jax.random.fold_in(key, 6), dim), (blocks,), jnp.float32, smallest / len(shards), top_value / len(shards))
        return jnp.repeat(jnp.exp(draws), shape[dim] // blocks).reshape((-1,) + (1,) * (len(shape) - dim - 1))

    gain = one(*shards[0])
    for cut in shards[1:]:
        gain = gain * one(*cut)
    return gain


def rank_table(count, slope):
    loads = [(1 << 20) // math.isqrt(rank ** slope) + 1 for rank in range(1, count + 1)]
    scale = 1 + sum(loads) // (1 << 30)
    return np.cumsum(np.array([max(1, weight // scale) for weight in loads]))


def skewed_ids(key, dims, amount, lean):
    grid = rank_table(amount, lean)
    pick = jax.random.randint(jax.random.fold_in(key, 1), dims, 0, int(grid[amount - 1]))
    rank = jnp.searchsorted(jnp.asarray(grid, jnp.int32), pick, side="right")
    return jax.random.permutation(jax.random.fold_in(key, 2), amount)[rank].astype(jnp.int32)


def normal_values(own_key, dims, scale, bound, cuts=(), kind=jnp.bfloat16):
    gain = steps_of(own_key, dims, cuts, -0.22, 0.18) if cuts else 1.0
    values = jax.random.normal(own_key, dims, jnp.float32) * scale * gain
    return jnp.minimum(jnp.maximum(values, -bound), bound).astype(kind)


def setup_inputs(seed: int = 0) -> dict:
    splits = jax.random.split(jax.random.key(seed), 8)
    ids = with_ends(skewed_ids(splits[0], (BATCH, F, BAG), VOCAB, 1), jax.random.fold_in(splits[0], 3), 0, VOCAB - 1).astype(jnp.int32)
    lengths = with_ends(jax.random.randint(splits[1], (BATCH, F), 1, BAG + 1), jax.random.fold_in(splits[1], 1), 1, BAG).astype(jnp.int32)
    tables = normal_values(splits[2], (F, VOCAB, E), 0.35, 5.0, ((0, 64), (1, 2)))
    cross_down = normal_values(splits[3], (FE, R), FE ** -0.5, 0.0234375, ((0, 2),))
    cross_up = normal_values(splits[4], (R, FE), R ** -0.5, 0.375, ((1, 2),))
    bias = normal_values(splits[5], (FE,), 0.5, 4.0, ((0, 2),), jnp.float32)
    grad_out = normal_values(splits[6], (BATCH, FE), 0.25, 4.0, ((0, 64), (1, 2)))
    return {"ids": ids, "lengths": lengths, "tables": tables, "cross_down": cross_down, "cross_up": cross_up, "bias": bias, "grad_out": grad_out}


def pool_feature(items):
    ids_f, live_f, table_f = items
    picked = table_f.astype(jnp.float32)[ids_f]
    return jnp.sum(picked * live_f[:, :, None], axis=1)


def grad_feature(items):
    ids_f, live_f, grad_f = items
    terms = grad_f[:, None, :] * live_f[:, :, None]
    total = jnp.zeros((VOCAB, E), jnp.float32)
    total = total.at[ids_f.reshape(-1)].add(terms.reshape(-1, E))
    return total.astype(jnp.bfloat16)


def reference(ids, lengths, tables, cross_down, cross_up, bias, grad_out):
    positions = jnp.arange(BAG, dtype=jnp.int32)
    live = (positions[None, None, :] < lengths[:, :, None]).astype(jnp.float32)
    ids_t = jnp.transpose(ids, (1, 0, 2))
    live_t = jnp.transpose(live, (1, 0, 2))
    pooled = lax.map(pool_feature, (ids_t, live_t, tables))
    x0 = pooled.astype(jnp.bfloat16).reshape(N_TABLE, N_ROW, PAIR, BATCH, E)
    x0 = jnp.transpose(x0, (3, 1, 0, 2, 4)).reshape(BATCH, FE)
    low = jnp.dot(x0, cross_down, preferred_element_type=jnp.float32).astype(jnp.bfloat16)
    gate = jnp.dot(low, cross_up, preferred_element_type=jnp.float32) + bias
    x0f = x0.astype(jnp.float32)
    crossed = (x0f * gate + x0f).astype(jnp.bfloat16)
    upstream = grad_out.astype(jnp.float32)
    dgate = (upstream * x0f).astype(jnp.bfloat16)
    dlow = jnp.dot(dgate, cross_up.T, preferred_element_type=jnp.float32).astype(jnp.bfloat16)
    x0_grad = upstream * gate + upstream + jnp.dot(dlow, cross_down.T, preferred_element_type=jnp.float32)
    x0_grad = x0_grad.astype(jnp.bfloat16).reshape(BATCH, N_ROW, N_TABLE, PAIR, E)
    back = jnp.transpose(x0_grad, (2, 1, 3, 0, 4)).reshape(F, BATCH, E).astype(jnp.float32)
    table_grad = lax.map(grad_feature, (ids_t, live_t, back))
    return crossed, table_grad
```

```python
import jax
import jax.numpy as jnp
from jax import lax
from jax.experimental import pallas as pl
from jax.experimental.pallas import tpu as pltpu
from jax.sharding import PartitionSpec as P

FIELDS = 8
BITS = 4
LANES = 128


def count_kernel(shard_ref, ids_ref, lengths_ref, packed_ref):
    feat = shard_ref[0] * packed_ref.shape[0]
    tables, rows, batch = packed_ref.shape
    bag = ids_ref.shape[1]
    slot = lax.broadcasted_iota(jnp.int32, (bag, LANES), 0)
    table_row = lax.broadcasted_iota(jnp.int32, (rows, LANES), 0)
    for k in range(tables):
        for start in range(0, batch, LANES):
            cols = pl.ds(start, LANES)
            ids = ids_ref[feat + k, :, cols]
            length = lengths_ref[k : k + 1, cols]
            for other in range(1, lengths_ref.shape[0] // tables):
                at = other * tables + k
                length = jnp.where(shard_ref[0] == other, lengths_ref[at : at + 1, cols], length)
            live = slot < length
            row = jnp.where(live, ids & (rows - 1), -1)
            unit = jnp.left_shift(1, lax.shift_right_logical(ids, rows.bit_length() - 1) * BITS)
            total = jnp.zeros((rows, LANES), jnp.int32)
            for p in range(bag):
                total = total + jnp.where(table_row == row[p : p + 1], unit[p : p + 1], 0)
            packed_ref[k, :, cols] = total


def count(shard, ids, lengths, tables, vocab):
    feats, bag, batch = ids.shape
    rows = vocab // FIELDS
    chunk = 512
    return pl.pallas_call(
        count_kernel,
        grid_spec=pltpu.PrefetchScalarGridSpec(
            num_scalar_prefetch=1,
            grid=(batch // chunk,),
            in_specs=[
                pl.BlockSpec((feats, bag, chunk), lambda b, s: (0, 0, b)),
                pl.BlockSpec((feats, chunk), lambda b, s: (0, b)),
            ],
            out_specs=pl.BlockSpec((tables, rows, chunk), lambda b, s: (0, 0, b)),
        ),
        out_shape=jax.ShapeDtypeStruct((tables, rows, batch), jnp.int32),
        cost_estimate=pl.CostEstimate(
            flops=3 * tables * rows * bag * batch,
            bytes_accessed=4 * batch * (feats * bag + tables * rows),
            transcendentals=0,
        ),
        name="count",
    )(shard, ids, lengths)


def unpack(packed_ref, counts_ref):
    rows, batch = packed_ref.shape[1:]
    for start in range(0, batch, LANES):
        cols = pl.ds(start, LANES)
        packed = packed_ref[0, :, cols]
        for j in range(FIELDS):
            field = lax.shift_right_logical(packed, j * BITS) & ((1 << BITS) - 1)
            counts_ref[j * rows : (j + 1) * rows, cols] = field.astype(jnp.float32).astype(jnp.bfloat16)


def pool_kernel(packed_ref, tables_ref, pooled_ref, counts_ref):
    unpack(packed_ref, counts_ref)
    table = tables_ref[:, 0].reshape(counts_ref.shape[0], tables_ref.shape[3])
    out = lax.dot_general(
        table, counts_ref[...], (((0,), (0,)), ((), ())), preferred_element_type=jnp.float32
    )
    pooled_ref[...] = jnp.transpose(out).astype(jnp.bfloat16)


def pool(packed, tables):
    pair, rows, batch = packed.shape
    shards, _, part, width = tables.shape
    vocab = shards * part
    chunk = 1024
    return pl.pallas_call(
        pool_kernel,
        grid=(pair, batch // chunk),
        in_specs=[
            pl.BlockSpec((1, rows, chunk), lambda k, b: (k, 0, b)),
            pl.BlockSpec((shards, 1, part, width), lambda k, b: (0, k, 0, 0)),
        ],
        out_specs=pl.BlockSpec((chunk, width), lambda k, b: (b, k)),
        out_shape=jax.ShapeDtypeStruct((batch, pair * width), jnp.bfloat16),
        scratch_shapes=[pltpu.VMEM((vocab, chunk), jnp.bfloat16)],
        cost_estimate=pl.CostEstimate(
            flops=2 * pair * batch * vocab * width,
            bytes_accessed=4 * packed.size + 2 * batch * pair * width,
            transcendentals=0,
        ),
        name="pool",
    )(packed, tables)


def scatter_kernel(packed_ref, back_ref, grad_ref, counts_ref, total_ref):
    unpack(packed_ref, counts_ref)
    part = jnp.dot(counts_ref[...], back_ref[...], preferred_element_type=jnp.float32)
    step = pl.program_id(1)

    @pl.when(step == 0)
    def _():
        total_ref[...] = part

    @pl.when(step > 0)
    def _():
        total_ref[...] += part

    @pl.when(step == pl.num_programs(1) - 1)
    def _():
        shards, _, half, width = grad_ref.shape
        grad_ref[:, 0] = total_ref[...].astype(jnp.bfloat16).reshape(shards, half, width)


def scatter(packed, back, shards):
    pair, rows, batch = packed.shape
    vocab = rows * FIELDS
    width = back.shape[1] // pair
    chunk = 1024
    return pl.pallas_call(
        scatter_kernel,
        grid=(pair, batch // chunk),
        in_specs=[
            pl.BlockSpec((1, rows, chunk), lambda k, b: (k, 0, b)),
            pl.BlockSpec((chunk, width), lambda k, b: (b, k)),
        ],
        out_specs=pl.BlockSpec((shards, 1, vocab // shards, width), lambda k, b: (0, k, 0, 0)),
        out_shape=jax.ShapeDtypeStruct((shards, pair, vocab // shards, width), jnp.bfloat16),
        scratch_shapes=[
            pltpu.VMEM((vocab, chunk), jnp.bfloat16),
            pltpu.VMEM((vocab, width), jnp.float32),
        ],
        cost_estimate=pl.CostEstimate(
            flops=2 * pair * batch * vocab * width,
            bytes_accessed=4 * packed.size + 2 * back.size,
            transcendentals=0,
        ),
        name="scatter",
    )(packed, back)


def project_kernel(x0_ref, down_ref, up_ref, grad_ref, sums_ref):
    groups, samples, cols = x0_ref.shape
    low = jnp.zeros((samples, down_ref.shape[1]), jnp.float32)
    dlow = jnp.zeros((samples, down_ref.shape[1]), jnp.float32)
    for g in range(groups):
        span = slice(g * cols, (g + 1) * cols)
        x0 = x0_ref[g]
        low += jnp.dot(x0, down_ref[span, :], preferred_element_type=jnp.float32)
        dgate = (grad_ref[:, span].astype(jnp.float32) * x0.astype(jnp.float32)).astype(jnp.bfloat16)
        dlow += lax.dot_general(
            dgate, up_ref[:, span], (((1,), (1,)), ((), ())), preferred_element_type=jnp.float32
        )

    @pl.when(pl.program_id(0) == 0)
    def _():
        sums_ref[:samples] = low
        sums_ref[samples:] = dlow

    @pl.when(pl.program_id(0) > 0)
    def _():
        sums_ref[:samples] += low
        sums_ref[samples:] += dlow


def project(x0, down, up, grad):
    count_, samples, cols = x0.shape
    rank = down.shape[1]
    groups = 4
    return pl.pallas_call(
        project_kernel,
        grid=(count_ // groups,),
        in_specs=[
            pl.BlockSpec((groups, samples, cols), lambda i: (i, 0, 0)),
            pl.BlockSpec((groups * cols, rank), lambda i: (i, 0)),
            pl.BlockSpec((rank, groups * cols), lambda i: (0, i)),
            pl.BlockSpec((samples, groups * cols), lambda i: (0, i)),
        ],
        out_specs=pl.BlockSpec((2 * samples, rank), lambda i: (0, 0)),
        out_shape=jax.ShapeDtypeStruct((2 * samples, rank), jnp.float32),
        cost_estimate=pl.CostEstimate(
            flops=4 * x0.size * rank, bytes_accessed=4 * x0.size + 4 * down.size, transcendentals=0
        ),
        name="project",
    )(x0, down, up, grad)


def cross_kernel(mine_ref, other_ref, x0_ref, down_ref, up_ref, bias_ref, grad_ref, crossed_ref, back_ref):
    groups, samples, cols = x0_ref.shape
    sums = (mine_ref[...] + other_ref[...]).astype(jnp.bfloat16)
    low, dlow = sums[:samples], sums[samples:]
    for g in range(groups):
        span = slice(g * cols, (g + 1) * cols)
        gate = jnp.dot(low, up_ref[:, span], preferred_element_type=jnp.float32) + bias_ref[:, span]
        spread = lax.dot_general(
            dlow, down_ref[span, :], (((1,), (1,)), ((), ())), preferred_element_type=jnp.float32
        )
        x0 = x0_ref[g].astype(jnp.float32)
        upstream = grad_ref[:, span].astype(jnp.float32)
        crossed_ref[:, span] = (x0 * gate + x0).astype(jnp.bfloat16)
        back_ref[g] = (upstream * gate + upstream + spread).astype(jnp.bfloat16)


def cross(mine, other, x0, down, up, bias, grad):
    count_, samples, cols = x0.shape
    rank = down.shape[1]
    groups = 4
    whole = pl.BlockSpec((2 * samples, rank), lambda i: (0, 0))
    return pl.pallas_call(
        cross_kernel,
        grid=(count_ // groups,),
        in_specs=[
            whole,
            whole,
            pl.BlockSpec((groups, samples, cols), lambda i: (i, 0, 0)),
            pl.BlockSpec((groups * cols, rank), lambda i: (i, 0)),
            pl.BlockSpec((rank, groups * cols), lambda i: (0, i)),
            pl.BlockSpec((1, groups * cols), lambda i: (0, i)),
            pl.BlockSpec((samples, groups * cols), lambda i: (0, i)),
        ],
        out_specs=[
            pl.BlockSpec((samples, groups * cols), lambda i: (0, i)),
            pl.BlockSpec((groups, samples, cols), lambda i: (i, 0, 0)),
        ],
        out_shape=[
            jax.ShapeDtypeStruct((samples, count_ * cols), jnp.bfloat16),
            jax.ShapeDtypeStruct((count_, samples, cols), jnp.bfloat16),
        ],
        cost_estimate=pl.CostEstimate(
            flops=4 * x0.size * rank, bytes_accessed=8 * x0.size + 4 * down.size, transcendentals=0
        ),
        name="cross",
    )(mine, other, x0, down, up, bias, grad)


def body(ids, lengths, tables, cross_down, cross_up, bias, grad_out):
    batch, feats, bag = ids.shape
    part, width = tables.shape[1:]
    shards = lax.axis_size("row")
    owners = lax.axis_size("table")
    pair = feats // shards
    vocab = shards * part
    shard = lax.axis_index("row").astype(jnp.int32).reshape(1)
    owned = lax.all_to_all(
        tables.reshape(shards, pair, part, width), "row", split_axis=0, concat_axis=0, tiled=True
    )
    packed = count(shard, jnp.transpose(ids, (1, 2, 0)), jnp.transpose(lengths), pair, vocab)
    pooled = pool(packed, owned)
    x0 = lax.all_to_all(
        pooled.reshape(owners, batch // owners, pair * width), "table", split_axis=0, concat_axis=0, tiled=True
    )
    mine = project(x0, cross_down, cross_up, grad_out)
    other = lax.ppermute(mine, "row", [(0, 1), (1, 0)])
    crossed, x0_grad = cross(mine, other, x0, cross_down, cross_up, bias.reshape(1, -1), grad_out)
    back = lax.all_to_all(x0_grad, "table", split_axis=0, concat_axis=0, tiled=True)
    halves = scatter(packed, back.reshape(batch, pair * width), shards)
    table_grad = lax.all_to_all(halves, "row", split_axis=0, concat_axis=0, tiled=True)
    return (crossed, table_grad.reshape(feats, part, width))


def solution(mesh):
    in_specs = (
        P(None, "table", None),
        P(None, "table"),
        P("table", "row", None),
        P("row", None),
        P(None, "row"),
        P("row"),
        P("table", "row"),
    )
    out_specs = (P("table", "row"), P("table", "row", None))
    return jax.shard_map(body, mesh=mesh, in_specs=in_specs, out_specs=out_specs, check_vma=False)
```

```python
import jax
import jax.numpy as jnp
from jax import lax
from jax.experimental import pallas as pl
from jax.experimental.pallas import tpu as pltpu
from jax.sharding import PartitionSpec as P

FIELDS = 8
BITS = 4
LANES = 128
MIB = 1 << 20


def count_kernel(shard_ref, ids_ref, lengths_ref, counts_ref):
    tables, vocab, batch = counts_ref.shape
    bag = ids_ref.shape[1]
    rows = vocab // FIELDS
    feat = shard_ref[0] * tables
    slot = lax.broadcasted_iota(jnp.int32, (bag, LANES), 0)
    table_row = lax.broadcasted_iota(jnp.int32, (rows, LANES), 0)
    for k in range(tables):
        for start in range(0, batch, LANES):
            cols = pl.ds(start, LANES)
            ids = ids_ref[feat + k, :, cols]
            length = lengths_ref[k : k + 1, cols]
            for other in range(1, lengths_ref.shape[0] // tables):
                at = other * tables + k
                length = jnp.where(shard_ref[0] == other, lengths_ref[at : at + 1, cols], length)
            row = jnp.where(slot < length, ids & (rows - 1), -1)
            unit = jnp.left_shift(1, lax.shift_right_logical(ids, rows.bit_length() - 1) * BITS)
            total = jnp.zeros((rows, LANES), jnp.int32)
            for p in range(bag):
                total = total + jnp.where(table_row == row[p : p + 1], unit[p : p + 1], 0)
            for j in range(FIELDS):
                field = lax.shift_right_logical(total, j * BITS) & ((1 << BITS) - 1)
                counts_ref[k, j * rows : (j + 1) * rows, cols] = field.astype(jnp.float32).astype(jnp.bfloat16)


def count(shard, ids, lengths, tables, vocab):
    feats, bag, batch = ids.shape
    chunk = 512
    return pl.pallas_call(
        count_kernel,
        grid_spec=pltpu.PrefetchScalarGridSpec(
            num_scalar_prefetch=1,
            grid=(batch // chunk,),
            in_specs=[
                pl.BlockSpec((feats, bag, chunk), lambda b, s: (0, 0, b)),
                pl.BlockSpec((feats, chunk), lambda b, s: (0, b)),
            ],
            out_specs=pl.BlockSpec((tables, vocab, chunk), lambda b, s: (0, 0, b)),
        ),
        out_shape=jax.ShapeDtypeStruct((tables, vocab, batch), jnp.bfloat16),
        compiler_params=pltpu.CompilerParams(vmem_limit_bytes=12 * MIB),
        cost_estimate=pl.CostEstimate(
            flops=tables * vocab * bag * batch,
            bytes_accessed=4 * ids.size + 2 * tables * vocab * batch,
            transcendentals=0,
        ),
        name="count",
    )(shard, ids, lengths)


def pool_kernel(counts_ref, tables_ref, pooled_ref):
    shards, _, part, width = tables_ref.shape
    table = tables_ref[:, 0].reshape(shards * part, width)
    out = lax.dot_general(
        table, counts_ref[0], (((0,), (0,)), ((), ())), preferred_element_type=jnp.float32
    )
    pooled_ref[...] = jnp.transpose(out.astype(jnp.bfloat16))


def pool(counts, tables):
    pair, vocab, batch = counts.shape
    shards, _, part, width = tables.shape
    chunk = 2048
    return pl.pallas_call(
        pool_kernel,
        grid=(pair, batch // chunk),
        in_specs=[
            pl.BlockSpec((1, vocab, chunk), lambda k, b: (k, 0, b)),
            pl.BlockSpec((shards, 1, part, width), lambda k, b: (0, k, 0, 0)),
        ],
        out_specs=pl.BlockSpec((chunk, width), lambda k, b: (b, k)),
        out_shape=jax.ShapeDtypeStruct((batch, pair * width), jnp.bfloat16),
        compiler_params=pltpu.CompilerParams(vmem_limit_bytes=14 * MIB),
        cost_estimate=pl.CostEstimate(
            flops=2 * counts.size * width,
            bytes_accessed=2 * counts.size + 2 * batch * pair * width,
            transcendentals=0,
        ),
        name="pool",
    )(counts, tables)


def scatter_kernel(shard_ref, counts_ref, back_ref, grad_ref):
    grad_ref[0] = jnp.dot(counts_ref[0], back_ref[...], preferred_element_type=jnp.float32).astype(jnp.bfloat16)


def scatter(half, place, counts, back, shards, slots):
    pair, vocab, batch = counts.shape
    part = vocab // shards
    width = back.shape[1] // pair
    return pl.pallas_call(
        scatter_kernel,
        grid_spec=pltpu.PrefetchScalarGridSpec(
            num_scalar_prefetch=1,
            grid=(pair,),
            in_specs=[
                pl.BlockSpec((1, part, batch), lambda k, s: (k, s[0], 0)),
                pl.BlockSpec((batch, width), lambda k, s: (0, k)),
            ],
            out_specs=pl.BlockSpec((1, part, width), lambda k, s: (s[1] * pair + k, 0, 0)),
        ),
        out_shape=jax.ShapeDtypeStruct((slots, part, width), jnp.bfloat16),
        compiler_params=pltpu.CompilerParams(vmem_limit_bytes=14 * MIB),
        cost_estimate=pl.CostEstimate(
            flops=2 * counts.size // shards * width,
            bytes_accessed=2 * counts.size // shards + 2 * back.size,
            transcendentals=0,
        ),
        name="scatter",
    )(jnp.stack([half, place]), counts, back)


def project_kernel(x0_ref, down_ref, up_ref, grad_ref, sums_ref):
    groups, samples, cols = x0_ref.shape
    step = pl.program_id(0)
    span = pl.ds(pl.multiple_of(step * groups * cols, groups * cols), groups * cols)
    x0 = jnp.concatenate([x0_ref[g] for g in range(groups)], axis=1)
    low = jnp.dot(x0, down_ref[span, :], preferred_element_type=jnp.float32)
    dgate = (grad_ref[...].astype(jnp.float32) * x0.astype(jnp.float32)).astype(jnp.bfloat16)
    dlow = lax.dot_general(
        dgate, up_ref[:, span], (((1,), (1,)), ((), ())), preferred_element_type=jnp.float32
    )

    @pl.when(step == 0)
    def _():
        sums_ref[:samples] = low
        sums_ref[samples:] = dlow

    @pl.when(step > 0)
    def _():
        sums_ref[:samples] += low
        sums_ref[samples:] += dlow


def project(x0, down, up, grad):
    owners, samples, cols = x0.shape
    rank = down.shape[1]
    groups = 8
    held = pl.BlockSpec(memory_space=pltpu.VMEM)
    return pl.pallas_call(
        project_kernel,
        grid=(owners // groups,),
        in_specs=[
            pl.BlockSpec((groups, samples, cols), lambda i: (i, 0, 0)),
            held,
            held,
            pl.BlockSpec((samples, groups * cols), lambda i: (0, i)),
        ],
        out_specs=pl.BlockSpec((2 * samples, rank), lambda i: (0, 0)),
        out_shape=jax.ShapeDtypeStruct((2 * samples, rank), jnp.float32),
        compiler_params=pltpu.CompilerParams(vmem_limit_bytes=14 * MIB),
        cost_estimate=pl.CostEstimate(
            flops=4 * x0.size * rank, bytes_accessed=4 * x0.size, transcendentals=0
        ),
        name="project",
    )(x0, down, up, grad)


def cross_kernel(mine_ref, other_ref, x0_ref, down_ref, up_ref, bias_ref, grad_ref, crossed_ref, back_ref):
    groups, samples, cols = x0_ref.shape
    step = pl.program_id(0)
    span = pl.ds(pl.multiple_of(step * groups * cols, groups * cols), groups * cols)
    sums = (mine_ref[...] + other_ref[...]).astype(jnp.bfloat16)
    gate = jnp.dot(sums[:samples], up_ref[:, span], preferred_element_type=jnp.float32) + bias_ref[...]
    spread = lax.dot_general(
        sums[samples:], down_ref[span, :], (((1,), (1,)), ((), ())), preferred_element_type=jnp.float32
    )
    x0 = jnp.concatenate([x0_ref[g] for g in range(groups)], axis=1).astype(jnp.float32)
    upstream = grad_ref[...].astype(jnp.float32)
    crossed_ref[...] = (x0 * gate + x0).astype(jnp.bfloat16)
    back = (upstream * gate + upstream + spread).astype(jnp.bfloat16)
    for g in range(groups):
        back_ref[g] = back[:, g * cols : (g + 1) * cols]


def cross(mine, other, x0, down, up, bias, grad):
    owners, samples, cols = x0.shape
    rank = down.shape[1]
    groups = 8
    whole = pl.BlockSpec((2 * samples, rank), lambda i: (0, 0))
    held = pl.BlockSpec(memory_space=pltpu.VMEM)
    return pl.pallas_call(
        cross_kernel,
        grid=(owners // groups,),
        in_specs=[
            whole,
            whole,
            pl.BlockSpec((groups, samples, cols), lambda i: (i, 0, 0)),
            held,
            held,
            pl.BlockSpec((1, groups * cols), lambda i: (0, i)),
            pl.BlockSpec((samples, groups * cols), lambda i: (0, i)),
        ],
        out_specs=[
            pl.BlockSpec((samples, groups * cols), lambda i: (0, i)),
            pl.BlockSpec((groups, samples, cols), lambda i: (i, 0, 0)),
        ],
        out_shape=[
            jax.ShapeDtypeStruct((samples, owners * cols), jnp.bfloat16),
            jax.ShapeDtypeStruct((owners, samples, cols), jnp.bfloat16),
        ],
        compiler_params=pltpu.CompilerParams(vmem_limit_bytes=20 * MIB),
        cost_estimate=pl.CostEstimate(
            flops=4 * x0.size * rank, bytes_accessed=8 * x0.size, transcendentals=0
        ),
        name="cross",
    )(mine, other, x0, down, up, bias, grad)


def body(ids, lengths, tables, cross_down, cross_up, bias, grad_out):
    batch, feats, bag = ids.shape
    part, width = tables.shape[1:]
    shards = lax.axis_size("row")
    owners = lax.axis_size("table")
    pair = feats // shards
    vocab = shards * part
    shard = lax.axis_index("row").astype(jnp.int32)
    swap = [(0, 1), (1, 0)]
    owned = lax.all_to_all(
        tables.reshape(shards, pair, part, width), "row", split_axis=0, concat_axis=0, tiled=True
    )
    counts = count(shard.reshape(1), jnp.transpose(ids, (1, 2, 0)), jnp.transpose(lengths), pair, vocab)
    pooled = pool(counts, owned)
    x0 = lax.all_to_all(
        pooled.reshape(owners, batch // owners, pair * width), "table", split_axis=0, concat_axis=0, tiled=True
    )
    down = pltpu.with_memory_space_constraint(cross_down, pltpu.VMEM)
    up = pltpu.with_memory_space_constraint(cross_up, pltpu.VMEM)
    mine = project(x0, down, up, grad_out)
    other = lax.ppermute(mine, "row", swap)
    crossed, x0_grad = cross(mine, other, x0, down, up, bias.reshape(1, -1), grad_out)
    back = lax.all_to_all(x0_grad, "table", split_axis=0, concat_axis=0, tiled=True)
    back = back.reshape(batch, pair * width)
    outgoing = scatter(1 - shard, jnp.zeros_like(shard), counts, back, shards, pair)
    incoming = lax.ppermute(outgoing, "row", swap)
    own = scatter(shard, shard, counts, back, shards, feats)
    table_grad = lax.dynamic_update_slice_in_dim(own, incoming, (1 - shard) * pair, 0)
    return (crossed, table_grad)


def solution(mesh):
    in_specs = (
        P(None, "table", None),
        P(None, "table"),
        P("table", "row", None),
        P("row", None),
        P(None, "row"),
        P("row"),
        P("table", "row"),
    )
    out_specs = (P("table", "row"), P("table", "row", None))
    return jax.shard_map(body, mesh=mesh, in_specs=in_specs, out_specs=out_specs, check_vma=False)
```

```python
import jax
import jax.numpy as jnp
from jax import lax
from jax.experimental import pallas as pl
from jax.experimental.pallas import tpu as pltpu
from jax.sharding import PartitionSpec as P

FIELDS = 8
BITS = 4
LANES = 128
MIB = 1 << 20
AHEAD = 3
HELD = pl.BlockSpec(memory_space=pltpu.VMEM)
FAR = pl.BlockSpec(memory_space=pl.ANY)


def near(x):
    return pltpu.with_memory_space_constraint(x, pltpu.VMEM)


def far(x):
    return pltpu.with_memory_space_constraint(x, pltpu.HBM)


def params(mib):
    return pltpu.CompilerParams(vmem_limit_bytes=mib * MIB)


def cost(flops, moved):
    return pl.CostEstimate(flops=flops, bytes_accessed=moved, transcendentals=0)


def count_kernel(shard_ref, ids_ref, lengths_ref, counts_ref):
    tables, vocab = counts_ref.shape[:2]
    bag, batch = ids_ref.shape[1:]
    rows = vocab // FIELDS
    feat = shard_ref[0] * tables
    base = pl.program_id(0) * batch
    slot = lax.broadcasted_iota(jnp.int32, (bag, LANES), 0)
    table_row = lax.broadcasted_iota(jnp.int32, (rows, LANES), 0)
    for k in range(tables):
        for start in range(0, batch, LANES):
            cols = pl.ds(start, LANES)
            out = pl.ds(pl.multiple_of(base + start, LANES), LANES)
            ids = ids_ref[feat + k, :, cols]
            length = lengths_ref[k : k + 1, cols]
            for other in range(1, lengths_ref.shape[0] // tables):
                at = other * tables + k
                length = jnp.where(shard_ref[0] == other, lengths_ref[at : at + 1, cols], length)
            row = jnp.where(slot < length, ids & (rows - 1), -1)
            unit = jnp.left_shift(1, lax.shift_right_logical(ids, rows.bit_length() - 1) * BITS)
            total = jnp.zeros((rows, LANES), jnp.int32)
            for p in range(bag):
                total = total + jnp.where(table_row == row[p : p + 1], unit[p : p + 1], 0)
            for j in range(FIELDS):
                field = lax.shift_right_logical(total, j * BITS) & ((1 << BITS) - 1)
                counts_ref[k, j * rows : (j + 1) * rows, out] = field.astype(jnp.float32).astype(jnp.bfloat16)


def count(shard, ids, lengths, tables, vocab):
    feats, bag, batch = ids.shape
    chunk = 512
    return pl.pallas_call(
        count_kernel,
        grid_spec=pltpu.PrefetchScalarGridSpec(
            num_scalar_prefetch=1,
            grid=(batch // chunk,),
            in_specs=[
                pl.BlockSpec((feats, bag, chunk), lambda b, s: (0, 0, b)),
                pl.BlockSpec((feats, chunk), lambda b, s: (0, b)),
            ],
            out_specs=HELD,
        ),
        out_shape=pltpu.VMEM((tables, vocab, batch), jnp.bfloat16),
        compiler_params=params(8),
        cost_estimate=cost(tables * vocab * bag * batch, 4 * ids.size),
        name="count",
    )(shard, far(ids), far(lengths))


def pool_kernel(shard_ref, counts_ref, own_ref, other_ref, pooled_ref, saved_ref, sem):
    part, width = own_ref.shape[1:]
    owners, _, samples, _ = pooled_ref.shape
    chunk = owners * samples
    k, step = pl.program_id(0), pl.program_id(1)
    save = pltpu.make_async_copy(counts_ref, saved_ref, sem)

    @pl.when((k == 0) & (step == 0))
    def _():
        save.start()

    cols = pl.ds(pl.multiple_of(step * chunk, chunk), chunk)
    total = jnp.zeros((width, chunk), jnp.float32)
    for place, table_ref in ((shard_ref[0], own_ref), (1 - shard_ref[0], other_ref)):
        rows = pl.ds(pl.multiple_of(place * part, part), part)
        total += lax.dot_general(
            table_ref[0], counts_ref[k, rows, cols], (((0,), (0,)), ((), ())), preferred_element_type=jnp.float32
        )
    pooled_ref[:, 0] = jnp.transpose(total.astype(jnp.bfloat16)).reshape(owners, samples, width)

    @pl.when((k == pl.num_programs(0) - 1) & (step == pl.num_programs(1) - 1))
    def _():
        save.wait()


def pool(shard, counts, tables, other, owners):
    pair, vocab, batch = counts.shape
    part, width = tables.shape[1:]
    steps = 2
    return pl.pallas_call(
        pool_kernel,
        grid_spec=pltpu.PrefetchScalarGridSpec(
            num_scalar_prefetch=1,
            grid=(pair, steps),
            in_specs=[
                HELD,
                pl.BlockSpec((1, part, width), lambda k, b, s: (s[0] * pair + k, 0, 0)),
                pl.BlockSpec((1, part, width), lambda k, b, s: (k, 0, 0)),
            ],
            out_specs=[
                pl.BlockSpec((owners // steps, 1, batch // owners, width), lambda k, b, s: (b, k, 0, 0)),
                FAR,
            ],
            scratch_shapes=[pltpu.SemaphoreType.DMA],
        ),
        out_shape=[
            jax.ShapeDtypeStruct((owners, pair, batch // owners, width), jnp.bfloat16),
            pltpu.HBM(counts.shape, counts.dtype),
        ],
        compiler_params=params(10),
        cost_estimate=cost(2 * counts.size * width, 4 * counts.size),
        name="pool",
    )(shard, near(counts), tables, other)


def scatter_kernel(shard_ref, counts_ref, back_ref, grad_ref):
    owners, _, samples, width = back_ref.shape
    back = back_ref[:, 0].reshape(owners * samples, width)
    grad_ref[0] = jnp.dot(counts_ref[0], back, preferred_element_type=jnp.float32).astype(jnp.bfloat16)


def scatter(shard, counts, back, shards, away):
    pair, vocab, batch = counts.shape
    part = vocab // shards
    owners, _, samples, width = back.shape
    return pl.pallas_call(
        scatter_kernel,
        grid_spec=pltpu.PrefetchScalarGridSpec(
            num_scalar_prefetch=1,
            grid=(pair,),
            in_specs=[
                pl.BlockSpec((1, part, batch), lambda k, s: (k, 1 - s[0] if away else s[0], 0)),
                pl.BlockSpec((owners, 1, samples, width), lambda k, s: (0, k, 0, 0)),
            ],
            out_specs=pl.BlockSpec((1, part, width), lambda k, s: (k if away else s[0] * pair + k, 0, 0)),
        ),
        out_shape=jax.ShapeDtypeStruct((pair if away else shards * pair, part, width), jnp.bfloat16),
        compiler_params=params(12),
        cost_estimate=cost(2 * counts.size // shards * width, 2 * counts.size // shards + 2 * back.size),
        name="scatter",
    )(shard, far(counts), back)


def row_of(x0_ref):
    groups, tables = x0_ref.shape[:2]
    return jnp.concatenate([x0_ref[g, k] for g in range(groups) for k in range(tables)], axis=1)


def stream(weight_ref, held_ref, sems, piece, steps):
    step = pl.program_id(0)

    def copy(i):
        return pltpu.make_async_copy(weight_ref.at[piece(i)], held_ref.at[piece(i)], sems.at[i])

    @pl.when(step == 0)
    def _():
        for i in range(min(AHEAD, steps)):
            copy(i).start()

    @pl.when(step + AHEAD < steps)
    def _():
        copy(step + AHEAD).start()

    copy(step).wait()


def add_up(total_ref, part):
    @pl.when(pl.program_id(0) == 0)
    def _():
        total_ref[...] = part

    @pl.when(pl.program_id(0) > 0)
    def _():
        total_ref[...] += part


def dlow_kernel(x0_ref, grad_ref, up_ref, dlow_ref):
    dgate = (grad_ref[...].astype(jnp.float32) * row_of(x0_ref).astype(jnp.float32)).astype(jnp.bfloat16)
    add_up(dlow_ref, lax.dot_general(dgate, up_ref[...], (((1,), (1,)), ((), ())), preferred_element_type=jnp.float32))


def low_kernel(steps, x0_ref, down_ref, low_ref, held_ref, sems):
    groups, tables, _, cols = x0_ref.shape
    width = groups * tables * cols
    span = lambda i: pl.ds(pl.multiple_of(i * width, width), width)
    x0 = row_of(x0_ref)
    stream(down_ref, held_ref, sems, span, steps)
    add_up(low_ref, jnp.dot(x0, held_ref[span(pl.program_id(0)), :], preferred_element_type=jnp.float32))


def spread_kernel(groups_cols, mine_ref, other_ref, down_ref, spread_ref):
    span = pl.ds(pl.multiple_of(pl.program_id(0) * groups_cols, groups_cols), groups_cols)
    dlow = (mine_ref[...] + other_ref[...]).astype(jnp.bfloat16)
    spread_ref[:, span] = lax.dot_general(
        dlow, down_ref[span, :], (((1,), (1,)), ((), ())), preferred_element_type=jnp.float32
    )


def cross_kernel(mine_ref, other_ref, x0_ref, up_ref, bias_ref, grad_ref, spread_ref, crossed_ref, back_ref):
    groups, tables, _, cols = x0_ref.shape
    width = groups * tables * cols
    span = pl.ds(pl.multiple_of(pl.program_id(0) * width, width), width)
    low = (mine_ref[...] + other_ref[...]).astype(jnp.bfloat16)
    gate = jnp.dot(low, up_ref[...], preferred_element_type=jnp.float32) + bias_ref[...]
    x0 = row_of(x0_ref).astype(jnp.float32)
    crossed_ref[...] = (x0 * gate + x0).astype(jnp.bfloat16)
    upstream = grad_ref[...].astype(jnp.float32)
    back = (upstream * gate + upstream + spread_ref[:, span]).astype(jnp.bfloat16)
    for g in range(groups):
        for k in range(tables):
            at = (g * tables + k) * cols
            back_ref[g, k] = back[:, at : at + cols]


def cross_layer(x0, down, up, bias, grad):
    owners, tables, samples, cols = x0.shape
    rank = down.shape[1]
    groups = 8
    steps = owners // groups
    width = groups * tables * cols
    x0_spec = pl.BlockSpec((groups, tables, samples, cols), lambda i: (i, 0, 0, 0))
    row_spec = pl.BlockSpec((samples, width), lambda i: (0, i))
    up_spec = pl.BlockSpec((rank, width), lambda i: (0, i))
    sum_spec = pl.BlockSpec((samples, rank), lambda i: (0, 0))
    sum_shape = jax.ShapeDtypeStruct((samples, rank), jnp.float32)
    work = 2 * x0.size * rank
    swap = [(0, 1), (1, 0)]

    def call(kernel, in_specs, out_specs, out_shape, mib, moved, name, *operands, sems=0):
        return pl.pallas_call(
            kernel,
            grid=(steps,),
            in_specs=in_specs,
            out_specs=out_specs,
            out_shape=out_shape,
            scratch_shapes=[pltpu.SemaphoreType.DMA((sems,))] if sems else [],
            compiler_params=params(mib),
            cost_estimate=cost(work, moved),
            name=name,
        )(*operands)

    dlow = call(
        dlow_kernel, [x0_spec, row_spec, up_spec], sum_spec, sum_shape, 12, 2 * up.size + 4 * x0.size, "dlow",
        x0, grad, far(up),
    )
    dlow_other = lax.ppermute(dlow, "row", swap)
    low, down = call(
        lambda *refs: low_kernel(steps, *refs), [x0_spec, FAR], [sum_spec, HELD],
        [sum_shape, pltpu.VMEM(down.shape, down.dtype)], 8, 2 * down.size + 2 * x0.size, "low",
        x0, far(down), sems=steps,
    )
    low_other = lax.ppermute(low, "row", swap)
    spread = call(
        lambda *refs: spread_kernel(width, *refs), [sum_spec, sum_spec, HELD], HELD,
        pltpu.VMEM((samples, owners * tables * cols), jnp.float32), 6, 4 * x0.size, "spread",
        dlow, dlow_other, near(down),
    )
    return call(
        cross_kernel,
        [sum_spec, sum_spec, x0_spec, up_spec, pl.BlockSpec((1, width), lambda i: (0, i)), row_spec, HELD],
        [row_spec, x0_spec],
        [pltpu.HBM((samples, owners * tables * cols), jnp.bfloat16), pltpu.HBM(x0.shape, jnp.bfloat16)],
        16, 8 * x0.size, "cross",
        low, low_other, x0, far(up), bias, grad, near(spread),
    )


def body(ids, lengths, tables, cross_down, cross_up, bias, grad_out):
    batch, feats, bag = ids.shape
    part, width = tables.shape[1:]
    shards = lax.axis_size("row")
    owners = lax.axis_size("table")
    pair = feats // shards
    shard = lax.axis_index("row").astype(jnp.int32)
    mine = shard.reshape(1)
    swap = [(0, 1), (1, 0)]
    sent = lax.dynamic_slice_in_dim(tables, (1 - shard) * pair, pair, 0)
    other = lax.ppermute(sent, "row", swap)
    counts = count(mine, jnp.transpose(ids, (1, 2, 0)), jnp.transpose(lengths), pair, shards * part)
    pooled, counts = pool(mine, counts, tables, other, owners)
    x0 = lax.all_to_all(pooled, "table", split_axis=0, concat_axis=0, tiled=True)
    crossed, x0_grad = cross_layer(x0, cross_down, cross_up, bias.reshape(1, -1), grad_out)
    back = lax.all_to_all(x0_grad, "table", split_axis=0, concat_axis=0, tiled=True)
    outgoing = scatter(mine, counts, back, shards, True)
    incoming = lax.ppermute(outgoing, "row", swap)
    own = scatter(mine, counts, back, shards, False)
    table_grad = lax.dynamic_update_slice_in_dim(own, incoming, (1 - shard) * pair, 0)
    return (crossed, table_grad)


def solution(mesh):
    in_specs = (
        P(None, "table", None),
        P(None, "table"),
        P("table", "row", None),
        P("row", None),
        P(None, "row"),
        P("row"),
        P("table", "row"),
    )
    out_specs = (P("table", "row"), P("table", "row", None))
    return jax.shard_map(body, mesh=mesh, in_specs=in_specs, out_specs=out_specs, check_vma=False)
```

```python
import jax
import jax.numpy as jnp
from jax import lax
from jax.experimental import pallas as pl
from jax.experimental.pallas import tpu as pltpu
from jax.sharding import PartitionSpec as P

FIELDS = 8
BITS = 4
LANES = 128
MIB = 1 << 20
AHEAD = 3
HELD = pl.BlockSpec(memory_space=pltpu.VMEM)
FAR = pl.BlockSpec(memory_space=pl.ANY)


def near(x):
    return pltpu.with_memory_space_constraint(x, pltpu.VMEM)


def far(x):
    return pltpu.with_memory_space_constraint(x, pltpu.HBM)


def params(mib):
    return pltpu.CompilerParams(vmem_limit_bytes=mib * MIB)


def cost(flops, moved):
    return pl.CostEstimate(flops=flops, bytes_accessed=moved, transcendentals=0)


def count_kernel(shard_ref, ids_ref, lengths_ref, counts_ref):
    tables, vocab = counts_ref.shape[1:3]
    bag, batch = ids_ref.shape[1:]
    rows = vocab // FIELDS
    feat = shard_ref[0] * tables
    step = pl.program_id(0)
    slot = lax.broadcasted_iota(jnp.int32, (bag, LANES), 0)
    table_row = lax.broadcasted_iota(jnp.int32, (rows, LANES), 0)
    for k in range(tables):
        for start in range(0, batch, LANES):
            cols = pl.ds(start, LANES)
            ids = ids_ref[feat + k, :, cols]
            length = lengths_ref[k : k + 1, cols]
            for other in range(1, lengths_ref.shape[0] // tables):
                at = other * tables + k
                length = jnp.where(shard_ref[0] == other, lengths_ref[at : at + 1, cols], length)
            row = jnp.where(slot < length, ids & (rows - 1), -1)
            unit = jnp.left_shift(1, lax.shift_right_logical(ids, rows.bit_length() - 1) * BITS)
            total = jnp.zeros((rows, LANES), jnp.int32)
            for p in range(bag):
                total = total + jnp.where(table_row == row[p : p + 1], unit[p : p + 1], 0)
            for j in range(FIELDS):
                field = lax.shift_right_logical(total, j * BITS) & ((1 << BITS) - 1)
                counts_ref[step, k, j * rows : (j + 1) * rows, cols] = field.astype(jnp.float32).astype(jnp.bfloat16)


def count(shard, ids, lengths, tables, vocab):
    feats, bag, batch = ids.shape
    chunk = 512
    return pl.pallas_call(
        count_kernel,
        grid_spec=pltpu.PrefetchScalarGridSpec(
            num_scalar_prefetch=1,
            grid=(batch // chunk,),
            in_specs=[
                pl.BlockSpec((feats, bag, chunk), lambda b, s: (0, 0, b)),
                pl.BlockSpec((feats, chunk), lambda b, s: (0, b)),
            ],
            out_specs=HELD,
        ),
        out_shape=pltpu.VMEM((batch // chunk, tables, vocab, chunk), jnp.bfloat16),
        compiler_params=params(8),
        cost_estimate=cost(tables * vocab * bag * batch, 4 * ids.size),
        name="count",
    )(shard, far(ids), far(lengths))


def pool_kernel(shard_ref, counts_ref, own_ref, other_ref, pooled_ref, saved_ref, sem):
    part, width = own_ref.shape[1:]
    samples = pooled_ref.shape[2]
    chunk = counts_ref.shape[3]
    blocks = pooled_ref.shape[0] * samples // chunk
    k, step = pl.program_id(0), pl.program_id(1)
    save = pltpu.make_async_copy(counts_ref, saved_ref, sem)

    @pl.when((k == 0) & (step == 0))
    def _():
        save.start()

    for c in range(blocks):
        total = jnp.zeros((width, chunk), jnp.float32)
        for place, table_ref in ((shard_ref[0], own_ref), (1 - shard_ref[0], other_ref)):
            rows = pl.ds(pl.multiple_of(place * part, part), part)
            total += lax.dot_general(
                table_ref[0], counts_ref[step * blocks + c, k, rows, :], (((0,), (0,)), ((), ())),
                preferred_element_type=jnp.float32,
            )
        owned = jnp.transpose(total.astype(jnp.bfloat16)).reshape(chunk // samples, samples, width)
        pooled_ref[c * (chunk // samples) : (c + 1) * (chunk // samples), 0] = owned

    @pl.when((k == pl.num_programs(0) - 1) & (step == pl.num_programs(1) - 1))
    def _():
        save.wait()


def pool(shard, counts, tables, other, owners):
    chunks, pair, vocab, chunk = counts.shape
    batch = chunks * chunk
    part, width = tables.shape[1:]
    steps = 2
    return pl.pallas_call(
        pool_kernel,
        grid_spec=pltpu.PrefetchScalarGridSpec(
            num_scalar_prefetch=1,
            grid=(pair, steps),
            in_specs=[
                HELD,
                pl.BlockSpec((1, part, width), lambda k, b, s: (s[0] * pair + k, 0, 0)),
                pl.BlockSpec((1, part, width), lambda k, b, s: (k, 0, 0)),
            ],
            out_specs=[
                pl.BlockSpec((owners // steps, 1, batch // owners, width), lambda k, b, s: (b, k, 0, 0)),
                FAR,
            ],
            scratch_shapes=[pltpu.SemaphoreType.DMA],
        ),
        out_shape=[
            jax.ShapeDtypeStruct((owners, pair, batch // owners, width), jnp.bfloat16),
            pltpu.HBM(counts.shape, counts.dtype),
        ],
        compiler_params=params(10),
        cost_estimate=cost(2 * counts.size * width, 4 * counts.size),
        name="pool",
    )(shard, near(counts), tables, other)


def scatter_kernel(shard_ref, counts_ref, back_ref, grad_ref):
    owners, _, samples, width = back_ref.shape
    back = back_ref[:, 0].reshape(owners * samples, width)
    counts = jnp.concatenate([counts_ref[c, 0] for c in range(counts_ref.shape[0])], axis=1)
    grad_ref[0] = jnp.dot(counts, back, preferred_element_type=jnp.float32).astype(jnp.bfloat16)


def scatter(shard, counts, back, shards, away):
    chunks, pair, vocab, chunk = counts.shape
    part = vocab // shards
    owners, _, samples, width = back.shape
    return pl.pallas_call(
        scatter_kernel,
        grid_spec=pltpu.PrefetchScalarGridSpec(
            num_scalar_prefetch=1,
            grid=(pair,),
            in_specs=[
                pl.BlockSpec((chunks, 1, part, chunk), lambda k, s: (0, k, 1 - s[0] if away else s[0], 0)),
                pl.BlockSpec((owners, 1, samples, width), lambda k, s: (0, k, 0, 0)),
            ],
            out_specs=pl.BlockSpec((1, part, width), lambda k, s: (k if away else s[0] * pair + k, 0, 0)),
        ),
        out_shape=jax.ShapeDtypeStruct((pair if away else shards * pair, part, width), jnp.bfloat16),
        compiler_params=params(12),
        cost_estimate=cost(2 * counts.size // shards * width, 2 * counts.size // shards + 2 * back.size),
        name="scatter",
    )(shard, far(counts), back)


def row_of(x0_ref):
    groups, tables = x0_ref.shape[:2]
    return jnp.concatenate([x0_ref[g, k] for g in range(groups) for k in range(tables)], axis=1)


def stream(steps, copies):
    step = pl.program_id(0)

    @pl.when(step == 0)
    def _():
        for i in range(min(AHEAD, steps)):
            for copy in copies(i):
                copy.start()

    @pl.when(step + AHEAD < steps)
    def _():
        for copy in copies(step + AHEAD):
            copy.start()

    for copy in copies(step):
        copy.wait()


def project_kernel(steps, x0_ref, grad_ref, down_ref, up_ref, sums_ref, held_ref, ring_ref, down_sems, up_sems):
    samples, width = grad_ref.shape
    step = pl.program_id(0)
    span = lambda i: pl.ds(pl.multiple_of(i * width, width), width)

    def copies(i):
        slot = lax.rem(i, AHEAD + 1)
        return (
            pltpu.make_async_copy(down_ref.at[span(i), :], held_ref.at[span(i), :], down_sems.at[slot]),
            pltpu.make_async_copy(up_ref.at[:, span(i)], ring_ref.at[slot], up_sems.at[slot]),
        )

    x0 = row_of(x0_ref)
    dgate = (grad_ref[...].astype(jnp.float32) * x0.astype(jnp.float32)).astype(jnp.bfloat16)
    stream(steps, copies)
    low = jnp.dot(x0, held_ref[span(step), :], preferred_element_type=jnp.float32)
    up = ring_ref[lax.rem(step, AHEAD + 1)]
    dlow = lax.dot_general(dgate, up, (((1,), (1,)), ((), ())), preferred_element_type=jnp.float32)

    @pl.when(step == 0)
    def _():
        sums_ref[:samples] = low
        sums_ref[samples:] = dlow

    @pl.when(step > 0)
    def _():
        sums_ref[:samples] += low
        sums_ref[samples:] += dlow


def cross_kernel(
    steps, mine_ref, other_ref, x0_ref, down_ref, up_ref, bias_ref, grad_ref, crossed_ref, back_ref, ring_ref, sems
):
    groups, tables, samples, cols = x0_ref.shape
    width = groups * tables * cols
    step = pl.program_id(0)
    span = lambda i: pl.ds(pl.multiple_of(i * width, width), width)

    def copies(i):
        slot = lax.rem(i, AHEAD + 1)
        return (pltpu.make_async_copy(up_ref.at[:, span(i)], ring_ref.at[slot], sems.at[slot]),)

    sums = (mine_ref[...] + other_ref[...]).astype(jnp.bfloat16)
    spread = lax.dot_general(
        sums[samples:], down_ref[span(step), :], (((1,), (1,)), ((), ())), preferred_element_type=jnp.float32
    )
    stream(steps, copies)
    up = ring_ref[lax.rem(step, AHEAD + 1)]
    gate = jnp.dot(sums[:samples], up, preferred_element_type=jnp.float32) + bias_ref[...]
    x0 = row_of(x0_ref).astype(jnp.float32)
    crossed_ref[...] = (x0 * gate + x0).astype(jnp.bfloat16)
    upstream = grad_ref[...].astype(jnp.float32)
    back = (upstream * gate + upstream + spread).astype(jnp.bfloat16)
    for g in range(groups):
        for k in range(tables):
            at = (g * tables + k) * cols
            back_ref[g, k] = back[:, at : at + cols]


def cross_layer(x0, down, up, bias, grad):
    owners, tables, samples, cols = x0.shape
    rank = down.shape[1]
    groups = 8
    steps = owners // groups
    width = groups * tables * cols
    x0_spec = pl.BlockSpec((groups, tables, samples, cols), lambda i: (i, 0, 0, 0))
    row_spec = pl.BlockSpec((samples, width), lambda i: (0, i))
    sum_spec = pl.BlockSpec((2 * samples, rank), lambda i: (0, 0))
    ring = pltpu.VMEM((AHEAD + 1, rank, width), up.dtype)
    sems = pltpu.SemaphoreType.DMA((AHEAD + 1,))
    sums, held = pl.pallas_call(
        lambda *refs: project_kernel(steps, *refs),
        grid=(steps,),
        in_specs=[x0_spec, row_spec, FAR, FAR],
        out_specs=[sum_spec, HELD],
        out_shape=[jax.ShapeDtypeStruct((2 * samples, rank), jnp.float32), pltpu.VMEM(down.shape, down.dtype)],
        scratch_shapes=[ring, sems, sems],
        compiler_params=params(14),
        cost_estimate=cost(4 * x0.size * rank, 4 * down.size + 4 * x0.size),
        name="project",
    )(x0, grad, far(down), far(up))
    other = lax.ppermute(sums, "row", [(0, 1), (1, 0)])
    return pl.pallas_call(
        lambda *refs: cross_kernel(steps, *refs),
        grid=(steps,),
        in_specs=[sum_spec, sum_spec, x0_spec, HELD, FAR, pl.BlockSpec((1, width), lambda i: (0, i)), row_spec],
        out_specs=[row_spec, x0_spec],
        out_shape=[pltpu.HBM((samples, owners * tables * cols), jnp.bfloat16), pltpu.HBM(x0.shape, jnp.bfloat16)],
        scratch_shapes=[ring, sems],
        compiler_params=params(20),
        cost_estimate=cost(4 * x0.size * rank, 2 * up.size + 8 * x0.size),
        name="cross",
    )(sums, other, x0, near(held), far(up), bias, grad)


def body(ids, lengths, tables, cross_down, cross_up, bias, grad_out):
    batch, feats, bag = ids.shape
    part, width = tables.shape[1:]
    shards = lax.axis_size("row")
    owners = lax.axis_size("table")
    pair = feats // shards
    shard = lax.axis_index("row").astype(jnp.int32)
    mine = shard.reshape(1)
    swap = [(0, 1), (1, 0)]
    sent = lax.dynamic_slice_in_dim(tables, (1 - shard) * pair, pair, 0)
    other = lax.ppermute(sent, "row", swap)
    counts = count(mine, jnp.transpose(ids, (1, 2, 0)), jnp.transpose(lengths), pair, shards * part)
    pooled, counts = pool(mine, counts, tables, other, owners)
    x0 = lax.all_to_all(pooled, "table", split_axis=0, concat_axis=0, tiled=True)
    crossed, x0_grad = cross_layer(x0, cross_down, cross_up, bias.reshape(1, -1), grad_out)
    back = lax.all_to_all(x0_grad, "table", split_axis=0, concat_axis=0, tiled=True)
    outgoing = scatter(mine, counts, back, shards, True)
    incoming = lax.ppermute(outgoing, "row", swap)
    own = scatter(mine, counts, back, shards, False)
    table_grad = lax.dynamic_update_slice_in_dim(own, incoming, (1 - shard) * pair, 0)
    return (crossed, table_grad)


def solution(mesh):
    in_specs = (
        P(None, "table", None),
        P(None, "table"),
        P("table", "row", None),
        P("row", None),
        P(None, "row"),
        P("row"),
        P("table", "row"),
    )
    out_specs = (P("table", "row"), P("table", "row", None))
    return jax.shard_map(body, mesh=mesh, in_specs=in_specs, out_specs=out_specs, check_vma=False)
```

```python
import jax
import jax.numpy as jnp
from jax import lax
from jax.experimental import pallas as pl
from jax.experimental.pallas import tpu as pltpu
from jax.sharding import PartitionSpec as P

FIELDS = 8
BITS = 4
LANES = 128
MIB = 1 << 20
AHEAD = 3
HELD = pl.BlockSpec(memory_space=pltpu.VMEM)
FAR = pl.BlockSpec(memory_space=pl.ANY)


def near(x):
    return pltpu.with_memory_space_constraint(x, pltpu.VMEM)


def far(x):
    return pltpu.with_memory_space_constraint(x, pltpu.HBM)


def params(mib):
    return pltpu.CompilerParams(vmem_limit_bytes=mib * MIB)


def cost(flops, moved):
    return pl.CostEstimate(flops=flops, bytes_accessed=moved, transcendentals=0)


def count_kernel(shard_ref, ids_ref, lengths_ref, counts_ref):
    tables, vocab = counts_ref.shape[1:3]
    bag, batch = ids_ref.shape[1:]
    rows = vocab // FIELDS
    feat = shard_ref[0] * tables
    step = pl.program_id(0)
    slot = lax.broadcasted_iota(jnp.int32, (bag, LANES), 0)
    table_row = lax.broadcasted_iota(jnp.int32, (rows, LANES), 0)
    for k in range(tables):
        for start in range(0, batch, LANES):
            cols = pl.ds(start, LANES)
            ids = ids_ref[feat + k, :, cols]
            length = lengths_ref[k : k + 1, cols]
            for other in range(1, lengths_ref.shape[0] // tables):
                at = other * tables + k
                length = jnp.where(shard_ref[0] == other, lengths_ref[at : at + 1, cols], length)
            row = jnp.where(slot < length, ids & (rows - 1), -1)
            unit = jnp.left_shift(1, lax.shift_right_logical(ids, rows.bit_length() - 1) * BITS)
            total = jnp.zeros((rows, LANES), jnp.int32)
            for p in range(bag):
                total = total + jnp.where(table_row == row[p : p + 1], unit[p : p + 1], 0)
            for j in range(FIELDS):
                field = lax.shift_right_logical(total, j * BITS) & ((1 << BITS) - 1)
                counts_ref[step, k, j * rows : (j + 1) * rows, cols] = field.astype(jnp.float32).astype(jnp.bfloat16)


def count(shard, ids, lengths, tables, vocab):
    feats, bag, batch = ids.shape
    chunk = 512
    return pl.pallas_call(
        count_kernel,
        grid_spec=pltpu.PrefetchScalarGridSpec(
            num_scalar_prefetch=1,
            grid=(batch // chunk,),
            in_specs=[
                pl.BlockSpec((feats, bag, chunk), lambda b, s: (0, 0, b)),
                pl.BlockSpec((feats, chunk), lambda b, s: (0, b)),
            ],
            out_specs=HELD,
        ),
        out_shape=pltpu.VMEM((batch // chunk, tables, vocab, chunk), jnp.bfloat16),
        compiler_params=params(8),
        cost_estimate=cost(tables * vocab * bag * batch, 4 * ids.size),
        name="count",
    )(shard, far(ids), far(lengths))


def pool_kernel(shard_ref, counts_ref, own_ref, other_ref, pooled_ref):
    part, width = own_ref.shape[1:]
    samples = pooled_ref.shape[2]
    chunk = counts_ref.shape[3]
    blocks = pooled_ref.shape[0] * samples // chunk
    k, step = pl.program_id(0), pl.program_id(1)
    for c in range(blocks):
        total = jnp.zeros((width, chunk), jnp.float32)
        for place, table_ref in ((shard_ref[0], own_ref), (1 - shard_ref[0], other_ref)):
            rows = pl.ds(pl.multiple_of(place * part, part), part)
            total += lax.dot_general(
                table_ref[0], counts_ref[step * blocks + c, k, rows, :], (((0,), (0,)), ((), ())),
                preferred_element_type=jnp.float32,
            )
        owned = jnp.transpose(total.astype(jnp.bfloat16)).reshape(chunk // samples, samples, width)
        pooled_ref[c * (chunk // samples) : (c + 1) * (chunk // samples), 0] = owned


def pool(shard, counts, tables, other, owners):
    chunks, pair, vocab, chunk = counts.shape
    batch = chunks * chunk
    part, width = tables.shape[1:]
    steps = 2
    return pl.pallas_call(
        pool_kernel,
        grid_spec=pltpu.PrefetchScalarGridSpec(
            num_scalar_prefetch=1,
            grid=(pair, steps),
            in_specs=[
                HELD,
                pl.BlockSpec((1, part, width), lambda k, b, s: (s[0] * pair + k, 0, 0)),
                pl.BlockSpec((1, part, width), lambda k, b, s: (k, 0, 0)),
            ],
            out_specs=pl.BlockSpec((owners // steps, 1, batch // owners, width), lambda k, b, s: (b, k, 0, 0)),
        ),
        out_shape=jax.ShapeDtypeStruct((owners, pair, batch // owners, width), jnp.bfloat16),
        compiler_params=params(10),
        cost_estimate=cost(2 * counts.size * width, 4 * counts.size),
        name="pool",
    )(shard, near(counts), tables, other)


def scatter_kernel(away, shard_ref, counts_ref, back_ref, grad_ref):
    owners, _, samples, width = back_ref.shape
    back = back_ref[:, 0].reshape(owners * samples, width)
    part = grad_ref.shape[1]
    half = 1 - shard_ref[0] if away else shard_ref[0]
    rows = pl.ds(pl.multiple_of(half * part, part), part)
    k = pl.program_id(0)
    counts = jnp.concatenate([counts_ref[c, k, rows, :] for c in range(counts_ref.shape[0])], axis=1)
    grad_ref[0] = jnp.dot(counts, back, preferred_element_type=jnp.float32).astype(jnp.bfloat16)


def scatter(shard, counts, back, shards, away):
    chunks, pair, vocab, chunk = counts.shape
    part = vocab // shards
    owners, _, samples, width = back.shape
    return pl.pallas_call(
        lambda *refs: scatter_kernel(away, *refs),
        grid_spec=pltpu.PrefetchScalarGridSpec(
            num_scalar_prefetch=1,
            grid=(pair,),
            in_specs=[
                HELD,
                pl.BlockSpec((owners, 1, samples, width), lambda k, s: (0, k, 0, 0)),
            ],
            out_specs=pl.BlockSpec((1, part, width), lambda k, s: (k if away else s[0] * pair + k, 0, 0)),
        ),
        out_shape=jax.ShapeDtypeStruct((pair if away else shards * pair, part, width), jnp.bfloat16),
        compiler_params=params(12),
        cost_estimate=cost(2 * counts.size // shards * width, 2 * counts.size // shards + 2 * back.size),
        name="scatter",
    )(shard, near(counts), back)


def row_of(x0_ref):
    groups, tables = x0_ref.shape[:2]
    return jnp.concatenate([x0_ref[g, k] for g in range(groups) for k in range(tables)], axis=1)


def stream(steps, ahead, copies):
    step = pl.program_id(0)

    @pl.when(step == 0)
    def _():
        for i in range(min(ahead, steps)):
            for copy in copies(i):
                copy.start()

    @pl.when(step + ahead < steps)
    def _():
        for copy in copies(step + ahead):
            copy.start()

    for copy in copies(step):
        copy.wait()


def project_kernel(steps, x0_ref, grad_ref, down_ref, up_ref, sums_ref, rounded_ref, held_ref, ring_ref, down_sems, up_sems):
    samples, width = grad_ref.shape
    step = pl.program_id(0)
    span = lambda i: pl.ds(pl.multiple_of(i * width, width), width)

    def copies(i):
        slot = lax.rem(i, AHEAD + 1)
        return (
            pltpu.make_async_copy(down_ref.at[span(i), :], held_ref.at[span(i), :], down_sems.at[slot]),
            pltpu.make_async_copy(up_ref.at[:, span(i)], ring_ref.at[slot], up_sems.at[slot]),
        )

    x0 = row_of(x0_ref)
    dgate = (grad_ref[...].astype(jnp.float32) * x0.astype(jnp.float32)).astype(jnp.bfloat16)
    stream(steps, AHEAD, copies)
    low = jnp.dot(x0, held_ref[span(step), :], preferred_element_type=jnp.float32)
    up = ring_ref[lax.rem(step, AHEAD + 1)]
    dlow = lax.dot_general(dgate, up, (((1,), (1,)), ((), ())), preferred_element_type=jnp.float32)

    @pl.when(step == 0)
    def _():
        sums_ref[:samples] = low
        sums_ref[samples:] = dlow

    @pl.when(step > 0)
    def _():
        sums_ref[:samples] += low
        sums_ref[samples:] += dlow

    @pl.when(step == steps - 1)
    def _():
        rounded_ref[...] = sums_ref[...].astype(jnp.bfloat16)


def cross_kernel(
    steps, mine_ref, other_ref, x0_ref, down_ref, up_ref, bias_ref, grad_ref, crossed_ref, back_ref, ring_ref, sems
):
    groups, tables, samples, cols = x0_ref.shape
    width = groups * tables * cols
    step = pl.program_id(0)
    span = lambda i: pl.ds(pl.multiple_of(i * width, width), width)

    def copies(i):
        slot = lax.rem(i, 2)
        return (pltpu.make_async_copy(up_ref.at[:, span(i)], ring_ref.at[slot], sems.at[slot]),)

    sums = (mine_ref[...] + other_ref[...].astype(jnp.float32)).astype(jnp.bfloat16)
    spread = lax.dot_general(
        sums[samples:], down_ref[span(step), :], (((1,), (1,)), ((), ())), preferred_element_type=jnp.float32
    )
    stream(steps, 1, copies)
    up = ring_ref[lax.rem(step, 2)]
    gate = jnp.dot(sums[:samples], up, preferred_element_type=jnp.float32) + bias_ref[...]
    x0 = row_of(x0_ref).astype(jnp.float32)
    crossed_ref[...] = (x0 * gate + x0).astype(jnp.bfloat16)
    upstream = grad_ref[...].astype(jnp.float32)
    back = (upstream * gate + upstream + spread).astype(jnp.bfloat16)
    for g in range(groups):
        for k in range(tables):
            at = (g * tables + k) * cols
            back_ref[g, k] = back[:, at : at + cols]


def cross_layer(x0, down, up, bias, grad):
    owners, tables, samples, cols = x0.shape
    rank = down.shape[1]
    groups = 8
    steps = owners // groups
    width = groups * tables * cols
    x0_spec = pl.BlockSpec((groups, tables, samples, cols), lambda i: (i, 0, 0, 0))
    row_spec = pl.BlockSpec((samples, width), lambda i: (0, i))
    sum_spec = pl.BlockSpec((2 * samples, rank), lambda i: (0, 0))
    ring = pltpu.VMEM((AHEAD + 1, rank, width), up.dtype)
    sems = pltpu.SemaphoreType.DMA((AHEAD + 1,))
    sums, rounded, held = pl.pallas_call(
        lambda *refs: project_kernel(steps, *refs),
        grid=(steps,),
        in_specs=[x0_spec, row_spec, FAR, FAR],
        out_specs=[sum_spec, sum_spec, HELD],
        out_shape=[
            jax.ShapeDtypeStruct((2 * samples, rank), jnp.float32),
            jax.ShapeDtypeStruct((2 * samples, rank), jnp.bfloat16),
            pltpu.VMEM(down.shape, down.dtype),
        ],
        scratch_shapes=[ring, sems, sems],
        compiler_params=params(12),
        cost_estimate=cost(4 * x0.size * rank, 4 * down.size + 4 * x0.size),
        name="project",
    )(x0, grad, far(down), far(up))
    other = lax.ppermute(rounded, "row", [(0, 1), (1, 0)])
    return pl.pallas_call(
        lambda *refs: cross_kernel(steps, *refs),
        grid=(steps,),
        in_specs=[sum_spec, sum_spec, x0_spec, HELD, FAR, pl.BlockSpec((1, width), lambda i: (0, i)), row_spec],
        out_specs=[row_spec, x0_spec],
        out_shape=[pltpu.HBM((samples, owners * tables * cols), jnp.bfloat16), pltpu.HBM(x0.shape, jnp.bfloat16)],
        scratch_shapes=[pltpu.VMEM((2, rank, width), up.dtype), pltpu.SemaphoreType.DMA((2,))],
        compiler_params=params(16),
        cost_estimate=cost(4 * x0.size * rank, 2 * up.size + 8 * x0.size),
        name="cross",
    )(sums, other, x0, near(held), far(up), bias, grad)


def body(ids, lengths, tables, cross_down, cross_up, bias, grad_out):
    batch, feats, bag = ids.shape
    part, width = tables.shape[1:]
    shards = lax.axis_size("row")
    owners = lax.axis_size("table")
    pair = feats // shards
    shard = lax.axis_index("row").astype(jnp.int32)
    mine = shard.reshape(1)
    swap = [(0, 1), (1, 0)]
    sent = lax.dynamic_slice_in_dim(tables, (1 - shard) * pair, pair, 0)
    other = lax.ppermute(sent, "row", swap)
    counts = count(mine, jnp.transpose(ids, (1, 2, 0)), jnp.transpose(lengths), pair, shards * part)
    pooled = pool(mine, counts, tables, other, owners)
    x0 = lax.all_to_all(pooled, "table", split_axis=0, concat_axis=0, tiled=True)
    crossed, x0_grad = cross_layer(x0, cross_down, cross_up, bias.reshape(1, -1), grad_out)
    back = lax.all_to_all(x0_grad, "table", split_axis=0, concat_axis=0, tiled=True)
    outgoing = scatter(mine, counts, back, shards, True)
    incoming = lax.ppermute(outgoing, "row", swap)
    own = scatter(mine, counts, back, shards, False)
    table_grad = lax.dynamic_update_slice_in_dim(own, incoming, (1 - shard) * pair, 0)
    return (crossed, table_grad)


def solution(mesh):
    in_specs = (
        P(None, "table", None),
        P(None, "table"),
        P("table", "row", None),
        P("row", None),
        P(None, "row"),
        P("row"),
        P("table", "row"),
    )
    out_specs = (P("table", "row"), P("table", "row", None))
    return jax.shard_map(body, mesh=mesh, in_specs=in_specs, out_specs=out_specs, check_vma=False)
```

```python
import jax
import jax.numpy as jnp
from jax import lax
from jax.experimental import pallas as pl
from jax.experimental.pallas import tpu as pltpu
from jax.sharding import PartitionSpec as P

FIELDS = 8
BITS = 4
LANES = 128
MIB = 1 << 20
AHEAD = 3
HELD = pl.BlockSpec(memory_space=pltpu.VMEM)
FAR = pl.BlockSpec(memory_space=pl.ANY)


def near(x):
    return pltpu.with_memory_space_constraint(x, pltpu.VMEM)


def far(x):
    return pltpu.with_memory_space_constraint(x, pltpu.HBM)


def params(mib):
    return pltpu.CompilerParams(vmem_limit_bytes=mib * MIB)


def cost(flops, moved):
    return pl.CostEstimate(flops=flops, bytes_accessed=moved, transcendentals=0)


def count_kernel(shard_ref, ids_ref, lengths_ref, counts_ref):
    tables, vocab = counts_ref.shape[1:3]
    bag, batch = ids_ref.shape[1:]
    rows = vocab // FIELDS
    feat = shard_ref[0] * tables
    step = pl.program_id(0)
    slot = lax.broadcasted_iota(jnp.int32, (bag, LANES), 0)
    table_row = lax.broadcasted_iota(jnp.int32, (rows, LANES), 0)
    for k in range(tables):
        for start in range(0, batch, LANES):
            cols = pl.ds(start, LANES)
            ids = ids_ref[feat + k, :, cols]
            length = lengths_ref[k : k + 1, cols]
            for other in range(1, lengths_ref.shape[0] // tables):
                at = other * tables + k
                length = jnp.where(shard_ref[0] == other, lengths_ref[at : at + 1, cols], length)
            row = jnp.where(slot < length, ids & (rows - 1), -1)
            unit = jnp.left_shift(1, lax.shift_right_logical(ids, rows.bit_length() - 1) * BITS)
            total = jnp.zeros((rows, LANES), jnp.int32)
            for p in range(bag):
                total = total + jnp.where(table_row == row[p : p + 1], unit[p : p + 1], 0)
            for j in range(FIELDS):
                field = lax.shift_right_logical(total, j * BITS) & ((1 << BITS) - 1)
                counts_ref[step, k, j * rows : (j + 1) * rows, cols] = field.astype(jnp.float32).astype(jnp.bfloat16)


def count(shard, ids, lengths, tables, vocab):
    feats, bag, batch = ids.shape
    chunk = 512
    return pl.pallas_call(
        count_kernel,
        grid_spec=pltpu.PrefetchScalarGridSpec(
            num_scalar_prefetch=1,
            grid=(batch // chunk,),
            in_specs=[
                pl.BlockSpec((feats, bag, chunk), lambda b, s: (0, 0, b)),
                pl.BlockSpec((feats, chunk), lambda b, s: (0, b)),
            ],
            out_specs=HELD,
        ),
        out_shape=pltpu.VMEM((batch // chunk, tables, vocab, chunk), jnp.bfloat16),
        compiler_params=params(8),
        cost_estimate=cost(tables * vocab * bag * batch, 4 * ids.size),
        name="count",
    )(shard, far(ids), far(lengths))


def pool_kernel(shard_ref, counts_ref, own_ref, other_ref, pooled_ref):
    part, width = own_ref.shape[1:]
    samples = pooled_ref.shape[2]
    chunk = counts_ref.shape[3]
    blocks = pooled_ref.shape[0] * samples // chunk
    k, step = pl.program_id(0), pl.program_id(1)
    for c in range(blocks):
        total = jnp.zeros((width, chunk), jnp.float32)
        for place, table_ref in ((shard_ref[0], own_ref), (1 - shard_ref[0], other_ref)):
            rows = pl.ds(pl.multiple_of(place * part, part), part)
            total += lax.dot_general(
                table_ref[0], counts_ref[step * blocks + c, k, rows, :], (((0,), (0,)), ((), ())),
                preferred_element_type=jnp.float32,
            )
        owned = jnp.transpose(total.astype(jnp.bfloat16)).reshape(chunk // samples, samples, width)
        pooled_ref[c * (chunk // samples) : (c + 1) * (chunk // samples), 0] = owned


def pool(shard, counts, tables, other, owners):
    chunks, pair, vocab, chunk = counts.shape
    batch = chunks * chunk
    part, width = tables.shape[1:]
    steps = 2
    return pl.pallas_call(
        pool_kernel,
        grid_spec=pltpu.PrefetchScalarGridSpec(
            num_scalar_prefetch=1,
            grid=(pair, steps),
            in_specs=[
                HELD,
                pl.BlockSpec((1, part, width), lambda k, b, s: (s[0] * pair + k, 0, 0)),
                pl.BlockSpec((1, part, width), lambda k, b, s: (k, 0, 0)),
            ],
            out_specs=pl.BlockSpec((owners // steps, 1, batch // owners, width), lambda k, b, s: (b, k, 0, 0)),
        ),
        out_shape=jax.ShapeDtypeStruct((owners, pair, batch // owners, width), jnp.bfloat16),
        compiler_params=params(10),
        cost_estimate=cost(2 * counts.size * width, 4 * counts.size),
        name="pool",
    )(shard, near(counts), tables, other)


def scatter_kernel(first, away, shard_ref, counts_ref, back_ref, grad_ref):
    owners, _, samples, width = back_ref.shape
    back = back_ref[:, 0].reshape(owners * samples, width)
    part = grad_ref.shape[1]
    half = 1 - shard_ref[0] if away else shard_ref[0]
    rows = pl.ds(pl.multiple_of(half * part, part), part)
    k = first + pl.program_id(0)
    counts = jnp.concatenate([counts_ref[c, k, rows, :] for c in range(counts_ref.shape[0])], axis=1)
    grad_ref[0] = jnp.dot(counts, back, preferred_element_type=jnp.float32).astype(jnp.bfloat16)


def scatter(shard, counts, back, shards, first, last, away):
    chunks, pair, vocab, chunk = counts.shape
    part = vocab // shards
    owners, _, samples, width = back.shape
    return pl.pallas_call(
        lambda *refs: scatter_kernel(first, away, *refs),
        grid_spec=pltpu.PrefetchScalarGridSpec(
            num_scalar_prefetch=1,
            grid=(last - first,),
            in_specs=[
                HELD,
                pl.BlockSpec((owners, 1, samples, width), lambda k, s: (0, first + k, 0, 0)),
            ],
            out_specs=pl.BlockSpec((1, part, width), lambda k, s: (k if away else s[0] * pair + first + k, 0, 0)),
        ),
        out_shape=jax.ShapeDtypeStruct((last - first if away else shards * pair, part, width), jnp.bfloat16),
        compiler_params=params(12),
        cost_estimate=cost(2 * counts.size // shards * width, 2 * counts.size // shards + 2 * back.size),
        name="scatter",
    )(shard, near(counts), back)


def row_of(x0_ref, groups):
    first = pl.program_id(0) * groups
    tables = x0_ref.shape[1]
    return jnp.concatenate([x0_ref[first + g, k] for g in range(groups) for k in range(tables)], axis=1)


def stream(steps, ahead, copies):
    step = pl.program_id(0)

    @pl.when(step == 0)
    def _():
        for i in range(min(ahead, steps)):
            for copy in copies(i):
                copy.start()

    @pl.when(step + ahead < steps)
    def _():
        for copy in copies(step + ahead):
            copy.start()

    for copy in copies(step):
        copy.wait()


def project_kernel(steps, x0_ref, grad_ref, down_ref, up_ref, sums_ref, held_ref, ring_ref, down_sems, up_sems):
    samples = grad_ref.shape[0]
    width = grad_ref.shape[1] // steps
    step = pl.program_id(0)
    span = lambda i: pl.ds(pl.multiple_of(i * width, width), width)

    def copies(i):
        slot = lax.rem(i, AHEAD + 1)
        return (
            pltpu.make_async_copy(down_ref.at[span(i), :], held_ref.at[span(i), :], down_sems.at[slot]),
            pltpu.make_async_copy(up_ref.at[:, span(i)], ring_ref.at[slot], up_sems.at[slot]),
        )

    x0 = row_of(x0_ref, x0_ref.shape[0] // steps)
    dgate = (grad_ref[:, span(step)].astype(jnp.float32) * x0.astype(jnp.float32)).astype(jnp.bfloat16)
    stream(steps, AHEAD, copies)
    low = jnp.dot(x0, held_ref[span(step), :], preferred_element_type=jnp.float32)
    up = ring_ref[lax.rem(step, AHEAD + 1)]
    dlow = lax.dot_general(dgate, up, (((1,), (1,)), ((), ())), preferred_element_type=jnp.float32)

    @pl.when(step == 0)
    def _():
        sums_ref[:samples] = low
        sums_ref[samples:] = dlow

    @pl.when(step > 0)
    def _():
        sums_ref[:samples] += low
        sums_ref[samples:] += dlow


def cross_kernel(
    steps, mine_ref, other_ref, x0_ref, down_ref, up_ref, bias_ref, grad_ref, crossed_ref, back_ref, ring_ref, sems
):
    groups, tables, samples, cols = back_ref.shape
    width = groups * tables * cols
    step = pl.program_id(0)
    span = lambda i: pl.ds(pl.multiple_of(i * width, width), width)

    def copies(i):
        slot = lax.rem(i, 2)
        return (pltpu.make_async_copy(up_ref.at[:, span(i)], ring_ref.at[slot], sems.at[slot]),)

    sums = (mine_ref[...] + other_ref[...]).astype(jnp.bfloat16)
    spread = lax.dot_general(
        sums[samples:], down_ref[span(step), :], (((1,), (1,)), ((), ())), preferred_element_type=jnp.float32
    )
    stream(steps, 1, copies)
    up = ring_ref[lax.rem(step, 2)]
    gate = jnp.dot(sums[:samples], up, preferred_element_type=jnp.float32) + bias_ref[...]
    x0 = row_of(x0_ref, groups).astype(jnp.float32)
    crossed_ref[...] = (x0 * gate + x0).astype(jnp.bfloat16)
    upstream = grad_ref[:, span(step)].astype(jnp.float32)
    back = (upstream * gate + upstream + spread).astype(jnp.bfloat16)
    for g in range(groups):
        for k in range(tables):
            at = (g * tables + k) * cols
            back_ref[g, k] = back[:, at : at + cols]


def cross_layer(x0, down, up, bias, grad):
    owners, tables, samples, cols = x0.shape
    rank = down.shape[1]
    groups = 8
    steps = owners // groups
    width = groups * tables * cols
    x0_spec = pl.BlockSpec((groups, tables, samples, cols), lambda i: (i, 0, 0, 0))
    row_spec = pl.BlockSpec((samples, width), lambda i: (0, i))
    sum_spec = pl.BlockSpec((2 * samples, rank), lambda i: (0, 0))
    ring = pltpu.VMEM((AHEAD + 1, rank, width), up.dtype)
    sems = pltpu.SemaphoreType.DMA((AHEAD + 1,))
    sums, held = pl.pallas_call(
        lambda *refs: project_kernel(steps, *refs),
        grid=(steps,),
        in_specs=[HELD, HELD, FAR, FAR],
        out_specs=[sum_spec, HELD],
        out_shape=[jax.ShapeDtypeStruct((2 * samples, rank), jnp.float32), pltpu.VMEM(down.shape, down.dtype)],
        scratch_shapes=[ring, sems, sems],
        compiler_params=params(12),
        cost_estimate=cost(4 * x0.size * rank, 4 * down.size + 4 * x0.size),
        name="project",
    )(near(x0), near(grad), far(down), far(up))
    other = lax.ppermute(sums, "row", [(0, 1), (1, 0)])
    return pl.pallas_call(
        lambda *refs: cross_kernel(steps, *refs),
        grid=(steps,),
        in_specs=[sum_spec, sum_spec, HELD, HELD, FAR, pl.BlockSpec((1, width), lambda i: (0, i)), HELD],
        out_specs=[row_spec, x0_spec],
        out_shape=[pltpu.HBM((samples, owners * tables * cols), jnp.bfloat16), pltpu.HBM(x0.shape, jnp.bfloat16)],
        scratch_shapes=[pltpu.VMEM((2, rank, width), up.dtype), pltpu.SemaphoreType.DMA((2,))],
        compiler_params=params(16),
        cost_estimate=cost(4 * x0.size * rank, 2 * up.size + 8 * x0.size),
        name="cross",
    )(sums, other, near(x0), near(held), far(up), bias, near(grad))


def body(ids, lengths, tables, cross_down, cross_up, bias, grad_out):
    batch, feats, bag = ids.shape
    part, width = tables.shape[1:]
    shards = lax.axis_size("row")
    owners = lax.axis_size("table")
    pair = feats // shards
    shard = lax.axis_index("row").astype(jnp.int32)
    mine = shard.reshape(1)
    swap = [(0, 1), (1, 0)]
    sent = lax.dynamic_slice_in_dim(tables, (1 - shard) * pair, pair, 0)
    other = lax.ppermute(sent, "row", swap)
    counts = count(mine, jnp.transpose(ids, (1, 2, 0)), jnp.transpose(lengths), pair, shards * part)
    pooled = pool(mine, counts, tables, other, owners)
    x0 = lax.all_to_all(pooled, "table", split_axis=0, concat_axis=0, tiled=True)
    crossed, x0_grad = cross_layer(x0, cross_down, cross_up, bias.reshape(1, -1), grad_out)
    back = lax.all_to_all(x0_grad, "table", split_axis=0, concat_axis=0, tiled=True)
    cuts = [0, pair // 2, pair]
    incoming = []
    for first, last in zip(cuts, cuts[1:]):
        outgoing = scatter(mine, counts, back, shards, first, last, True)
        incoming.append(lax.ppermute(outgoing, "row", swap))
    table_grad = scatter(mine, counts, back, shards, 0, pair, False)
    incoming = jnp.concatenate(incoming, axis=0)
    table_grad = lax.dynamic_update_slice_in_dim(table_grad, incoming, (1 - shard) * pair, 0)
    return (crossed, table_grad)


def solution(mesh):
    in_specs = (
        P(None, "table", None),
        P(None, "table"),
        P("table", "row", None),
        P("row", None),
        P(None, "row"),
        P("row"),
        P("table", "row"),
    )
    out_specs = (P("table", "row"), P("table", "row", None))
    return jax.shard_map(body, mesh=mesh, in_specs=in_specs, out_specs=out_specs, check_vma=False)
```

```python
import jax
import jax.numpy as jnp
from jax import lax
from jax.experimental import pallas as pl
from jax.experimental.pallas import tpu as pltpu
from jax.sharding import PartitionSpec as P

FIELDS = 8
BITS = 4
LANES = 128
MIB = 1 << 20
AHEAD = 2
HELD = pl.BlockSpec(memory_space=pltpu.VMEM)
FAR = pl.BlockSpec(memory_space=pl.ANY)


def near(x):
    return pltpu.with_memory_space_constraint(x, pltpu.VMEM)


def far(x):
    return pltpu.with_memory_space_constraint(x, pltpu.HBM)


def params(mib):
    return pltpu.CompilerParams(vmem_limit_bytes=mib * MIB)


def cost(flops, moved):
    return pl.CostEstimate(flops=flops, bytes_accessed=moved, transcendentals=0)


def count_kernel(shard_ref, ids_ref, lengths_ref, counts_ref):
    tables, vocab = counts_ref.shape[1:3]
    bag, batch = ids_ref.shape[1:]
    rows = vocab // FIELDS
    feat = shard_ref[0] * tables
    step = pl.program_id(0)
    slot = lax.broadcasted_iota(jnp.int32, (bag, LANES), 0)
    table_row = lax.broadcasted_iota(jnp.int32, (rows, LANES), 0)
    for k in range(tables):
        for start in range(0, batch, LANES):
            cols = pl.ds(start, LANES)
            ids = ids_ref[feat + k, :, cols]
            length = lengths_ref[k : k + 1, cols]
            for other in range(1, lengths_ref.shape[0] // tables):
                at = other * tables + k
                length = jnp.where(shard_ref[0] == other, lengths_ref[at : at + 1, cols], length)
            row = jnp.where(slot < length, ids & (rows - 1), -1)
            unit = jnp.left_shift(1, lax.shift_right_logical(ids, rows.bit_length() - 1) * BITS)
            total = jnp.zeros((rows, LANES), jnp.int32)
            for p in range(bag):
                total = total + jnp.where(table_row == row[p : p + 1], unit[p : p + 1], 0)
            for j in range(FIELDS):
                field = lax.shift_right_logical(total, j * BITS) & ((1 << BITS) - 1)
                counts_ref[step, k, j * rows : (j + 1) * rows, cols] = field.astype(jnp.float32).astype(jnp.bfloat16)


def count(shard, ids, lengths, tables, vocab):
    feats, bag, batch = ids.shape
    chunk = 512
    return pl.pallas_call(
        count_kernel,
        grid_spec=pltpu.PrefetchScalarGridSpec(
            num_scalar_prefetch=1,
            grid=(batch // chunk,),
            in_specs=[
                pl.BlockSpec((feats, bag, chunk), lambda b, s: (0, 0, b)),
                pl.BlockSpec((feats, chunk), lambda b, s: (0, b)),
            ],
            out_specs=HELD,
        ),
        out_shape=pltpu.VMEM((batch // chunk, tables, vocab, chunk), jnp.bfloat16),
        compiler_params=params(14),
        cost_estimate=cost(tables * vocab * bag * batch, 4 * ids.size),
        name="count",
    )(shard, far(ids), far(lengths))


def pool_kernel(shard_ref, counts_ref, own_ref, other_ref, weight_ref, pooled_ref, held_ref, sem):
    part, width = own_ref.shape[1:]
    samples = pooled_ref.shape[2]
    chunk = counts_ref.shape[3]
    blocks = pooled_ref.shape[0] * samples // chunk
    k, step = pl.program_id(0), pl.program_id(1)
    fetch = pltpu.make_async_copy(weight_ref.at[: held_ref.shape[0]], held_ref, sem)

    @pl.when((k == 0) & (step == 0))
    def _():
        fetch.start()

    for c in range(blocks):
        total = jnp.zeros((width, chunk), jnp.float32)
        for place, table_ref in ((shard_ref[0], own_ref), (1 - shard_ref[0], other_ref)):
            rows = pl.ds(pl.multiple_of(place * part, part), part)
            total += lax.dot_general(
                table_ref[0], counts_ref[step * blocks + c, k, rows, :], (((0,), (0,)), ((), ())),
                preferred_element_type=jnp.float32,
            )
        owned = jnp.transpose(total.astype(jnp.bfloat16)).reshape(chunk // samples, samples, width)
        pooled_ref[c * (chunk // samples) : (c + 1) * (chunk // samples), 0] = owned

    @pl.when((k == pl.num_programs(0) - 1) & (step == pl.num_programs(1) - 1))
    def _():
        fetch.wait()


def pool(shard, counts, tables, other, weight, owners):
    chunks, pair, vocab, chunk = counts.shape
    batch = chunks * chunk
    part, width = tables.shape[1:]
    steps = 2
    return pl.pallas_call(
        pool_kernel,
        grid_spec=pltpu.PrefetchScalarGridSpec(
            num_scalar_prefetch=1,
            grid=(pair, steps),
            in_specs=[
                HELD,
                pl.BlockSpec((1, part, width), lambda k, b, s: (s[0] * pair + k, 0, 0)),
                pl.BlockSpec((1, part, width), lambda k, b, s: (k, 0, 0)),
                FAR,
            ],
            out_specs=[
                pl.BlockSpec((owners // steps, 1, batch // owners, width), lambda k, b, s: (b, k, 0, 0)),
                HELD,
            ],
            scratch_shapes=[pltpu.SemaphoreType.DMA],
        ),
        out_shape=[
            jax.ShapeDtypeStruct((owners, pair, batch // owners, width), jnp.bfloat16),
            pltpu.VMEM((weight.shape[0] // 2, weight.shape[1]), weight.dtype),
        ],
        compiler_params=params(14),
        cost_estimate=cost(2 * counts.size * width, 4 * counts.size),
        name="pool",
    )(shard, near(counts), tables, other, far(weight))


def scatter_kernel(first, away, shard_ref, counts_ref, back_ref, grad_ref):
    owners, _, samples, width = back_ref.shape
    back = back_ref[:, 0].reshape(owners * samples, width)
    part = grad_ref.shape[1]
    half = 1 - shard_ref[0] if away else shard_ref[0]
    rows = pl.ds(pl.multiple_of(half * part, part), part)
    k = first + pl.program_id(0)
    counts = jnp.concatenate([counts_ref[c, k, rows, :] for c in range(counts_ref.shape[0])], axis=1)
    grad_ref[0] = jnp.dot(counts, back, preferred_element_type=jnp.float32).astype(jnp.bfloat16)


def scatter(shard, counts, back, shards, first, last, away):
    chunks, pair, vocab, chunk = counts.shape
    part = vocab // shards
    owners, _, samples, width = back.shape
    return pl.pallas_call(
        lambda *refs: scatter_kernel(first, away, *refs),
        grid_spec=pltpu.PrefetchScalarGridSpec(
            num_scalar_prefetch=1,
            grid=(last - first,),
            in_specs=[
                HELD,
                pl.BlockSpec((owners, 1, samples, width), lambda k, s: (0, first + k, 0, 0)),
            ],
            out_specs=pl.BlockSpec((1, part, width), lambda k, s: (k if away else s[0] * pair + first + k, 0, 0)),
        ),
        out_shape=jax.ShapeDtypeStruct((last - first if away else shards * pair, part, width), jnp.bfloat16),
        compiler_params=params(12),
        cost_estimate=cost(2 * counts.size // shards * width, 2 * counts.size // shards + 2 * back.size),
        name="scatter",
    )(shard, near(counts), back)


def row_of(x0_ref, groups):
    first = pl.program_id(0) * groups
    tables = x0_ref.shape[1]
    return jnp.concatenate([x0_ref[first + g, k] for g in range(groups) for k in range(tables)], axis=1)


def stream(steps, ahead, copies):
    step = pl.program_id(0)

    @pl.when(step == 0)
    def _():
        for i in range(min(ahead, steps)):
            for copy in copies(i):
                copy.start()

    @pl.when(step + ahead < steps)
    def _():
        for copy in copies(step + ahead):
            copy.start()

    for copy in copies(step):
        copy.wait()


def in_halves(steps, work, first_ref, second_ref):
    step = pl.program_id(0)
    half = steps // 2
    rows = first_ref.shape[0] // half

    @pl.when(step < half)
    def _():
        work(first_ref.at[pl.ds(pl.multiple_of(step * rows, rows), rows)])

    @pl.when(step >= half)
    def _():
        work(second_ref.at[pl.ds(pl.multiple_of((step - half) * rows, rows), rows)])


def project_kernel(
    steps, x0_ref, grad_ref, first_ref, down_ref, up_ref, sums_ref, second_ref, ring_ref, down_sems, sems
):
    samples = grad_ref.shape[0]
    width = grad_ref.shape[1] // steps
    half = steps // 2
    step = pl.program_id(0)
    span = lambda i: pl.ds(pl.multiple_of(i * width, width), width)

    def copies(i):
        slot = lax.rem(i, AHEAD + 1)
        return (pltpu.make_async_copy(up_ref.at[:, span(i)], ring_ref.at[slot], sems.at[slot]),)

    def second(i):
        return pltpu.make_async_copy(down_ref.at[span(half + i), :], second_ref.at[span(i), :], down_sems.at[i])

    stream(steps, AHEAD, copies)

    @pl.when(step < half)
    def _():
        second(step).start()

    @pl.when(step >= half)
    def _():
        second(step - half).wait()

    def work(weight_ref):
        x0 = row_of(x0_ref, x0_ref.shape[0] // steps)
        dgate = (grad_ref[:, span(step)].astype(jnp.float32) * x0.astype(jnp.float32)).astype(jnp.bfloat16)
        low = jnp.dot(x0, weight_ref[...], preferred_element_type=jnp.float32)
        up = ring_ref[lax.rem(step, AHEAD + 1)]
        dlow = lax.dot_general(dgate, up, (((1,), (1,)), ((), ())), preferred_element_type=jnp.float32)

        @pl.when(step == 0)
        def _():
            sums_ref[:samples] = low
            sums_ref[samples:] = dlow

        @pl.when(step > 0)
        def _():
            sums_ref[:samples] += low
            sums_ref[samples:] += dlow

    in_halves(steps, work, first_ref, second_ref)


def cross_kernel(
    steps, mine_ref, other_ref, x0_ref, first_ref, second_ref, up_ref, bias_ref, grad_ref, crossed_ref, back_ref, ring_ref, sems
):
    groups, tables, samples, cols = back_ref.shape
    width = groups * tables * cols
    step = pl.program_id(0)
    span = lambda i: pl.ds(pl.multiple_of(i * width, width), width)

    def copies(i):
        slot = lax.rem(i, 2)
        return (pltpu.make_async_copy(up_ref.at[:, span(i)], ring_ref.at[slot], sems.at[slot]),)

    def work(weight_ref):
        sums = (mine_ref[...] + other_ref[...]).astype(jnp.bfloat16)
        spread = lax.dot_general(
            sums[samples:], weight_ref[...], (((1,), (1,)), ((), ())), preferred_element_type=jnp.float32
        )
        stream(steps, 1, copies)
        up = ring_ref[lax.rem(step, 2)]
        gate = jnp.dot(sums[:samples], up, preferred_element_type=jnp.float32)
        scale = gate + (bias_ref[...] + 1.0)
        x0 = row_of(x0_ref, groups).astype(jnp.float32)
        crossed_ref[...] = (x0 * scale).astype(jnp.bfloat16)
        upstream = grad_ref[:, span(step)].astype(jnp.float32)
        back = (upstream * scale + spread).astype(jnp.bfloat16)
        for g in range(groups):
            for k in range(tables):
                at = (g * tables + k) * cols
                back_ref[g, k] = back[:, at : at + cols]

    in_halves(steps, work, first_ref, second_ref)


def cross_layer(x0, first, down, up, bias, grad):
    owners, tables, samples, cols = x0.shape
    rank = down.shape[1]
    groups = 8
    steps = owners // groups
    width = groups * tables * cols
    x0_spec = pl.BlockSpec((groups, tables, samples, cols), lambda i: (i, 0, 0, 0))
    row_spec = pl.BlockSpec((samples, width), lambda i: (0, i))
    sum_spec = pl.BlockSpec((2 * samples, rank), lambda i: (0, 0))
    ring = pltpu.VMEM((AHEAD + 1, rank, width), up.dtype)
    sems = pltpu.SemaphoreType.DMA((AHEAD + 1,))
    sums, second = pl.pallas_call(
        lambda *refs: project_kernel(steps, *refs),
        grid=(steps,),
        in_specs=[HELD, HELD, HELD, FAR, FAR],
        out_specs=[sum_spec, HELD],
        out_shape=[jax.ShapeDtypeStruct((2 * samples, rank), jnp.float32), pltpu.VMEM(first.shape, first.dtype)],
        scratch_shapes=[ring, pltpu.SemaphoreType.DMA((steps // 2,)), sems],
        compiler_params=params(14),
        cost_estimate=cost(4 * x0.size * rank, 2 * up.size + 4 * x0.size),
        name="project",
    )(near(x0), near(grad), near(first), far(down), far(up))
    other = lax.ppermute(sums, "row", [(0, 1), (1, 0)])
    return pl.pallas_call(
        lambda *refs: cross_kernel(steps, *refs),
        grid=(steps,),
        in_specs=[sum_spec, sum_spec, HELD, HELD, HELD, FAR, pl.BlockSpec((1, width), lambda i: (0, i)), HELD],
        out_specs=[row_spec, x0_spec],
        out_shape=[pltpu.HBM((samples, owners * tables * cols), jnp.bfloat16), pltpu.HBM(x0.shape, jnp.bfloat16)],
        scratch_shapes=[pltpu.VMEM((2, rank, width), up.dtype), pltpu.SemaphoreType.DMA((2,))],
        compiler_params=params(14),
        cost_estimate=cost(4 * x0.size * rank, 2 * up.size + 8 * x0.size),
        name="cross",
    )(sums, other, near(x0), near(first), near(second), far(up), bias, near(grad))


def body(ids, lengths, tables, cross_down, cross_up, bias, grad_out):
    batch, feats, bag = ids.shape
    part, width = tables.shape[1:]
    shards = lax.axis_size("row")
    owners = lax.axis_size("table")
    pair = feats // shards
    shard = lax.axis_index("row").astype(jnp.int32)
    mine = shard.reshape(1)
    swap = [(0, 1), (1, 0)]
    sent = lax.dynamic_slice_in_dim(tables, (1 - shard) * pair, pair, 0)
    other = lax.ppermute(sent, "row", swap)
    ids, lengths = jnp.transpose(ids, (1, 2, 0)), jnp.transpose(lengths)
    counts = count(mine, ids, lengths, pair, shards * part)
    pooled, first = pool(mine, counts, tables, other, cross_down, owners)
    x0 = lax.all_to_all(pooled, "table", split_axis=0, concat_axis=0, tiled=True)
    crossed, x0_grad = cross_layer(x0, first, cross_down, cross_up, bias.reshape(1, -1), grad_out)
    back = lax.all_to_all(x0_grad, "table", split_axis=0, concat_axis=0, tiled=True)
    cuts = [0, pair // 2, pair]
    incoming = []
    for first, last in zip(cuts, cuts[1:]):
        outgoing = scatter(mine, counts, back, shards, first, last, True)
        incoming.append(lax.ppermute(outgoing, "row", swap))
    table_grad = scatter(mine, counts, back, shards, 0, pair, False)
    incoming = jnp.concatenate(incoming, axis=0)
    table_grad = lax.dynamic_update_slice_in_dim(table_grad, incoming, (1 - shard) * pair, 0)
    return (crossed, table_grad)


def solution(mesh):
    in_specs = (
        P(None, "table", None),
        P(None, "table"),
        P("table", "row", None),
        P("row", None),
        P(None, "row"),
        P("row"),
        P("table", "row"),
    )
    out_specs = (P("table", "row"), P("table", "row", None))
    return jax.shard_map(body, mesh=mesh, in_specs=in_specs, out_specs=out_specs, check_vma=False)
```

```python
import jax
import jax.numpy as jnp
from jax import lax
from jax.experimental import pallas as pl
from jax.experimental.pallas import tpu as pltpu
from jax.sharding import PartitionSpec as P

FIELDS = 8
BITS = 4
LANES = 128
MIB = 1 << 20
AHEAD = 2
STEPS = 8
EARLY = 2
HELD = pl.BlockSpec(memory_space=pltpu.VMEM)
FAR = pl.BlockSpec(memory_space=pl.ANY)


def near(x):
    return pltpu.with_memory_space_constraint(x, pltpu.VMEM)


def far(x):
    return pltpu.with_memory_space_constraint(x, pltpu.HBM)


def params(mib):
    return pltpu.CompilerParams(vmem_limit_bytes=mib * MIB)


def cost(flops, moved):
    return pl.CostEstimate(flops=flops, bytes_accessed=moved, transcendentals=0)


def count_kernel(shard_ref, ids_ref, lengths_ref, counts_ref):
    tables, vocab = counts_ref.shape[1:3]
    bag, batch = ids_ref.shape[1:]
    rows = vocab // FIELDS
    feat = shard_ref[0] * tables
    step = pl.program_id(0)
    slot = lax.broadcasted_iota(jnp.int32, (bag, LANES), 0)
    table_row = lax.broadcasted_iota(jnp.int32, (rows, LANES), 0)
    for k in range(tables):
        for start in range(0, batch, LANES):
            cols = pl.ds(start, LANES)
            ids = ids_ref[feat + k, :, cols]
            length = lengths_ref[k : k + 1, cols]
            for other in range(1, lengths_ref.shape[0] // tables):
                at = other * tables + k
                length = jnp.where(shard_ref[0] == other, lengths_ref[at : at + 1, cols], length)
            row = jnp.where(slot < length, ids & (rows - 1), -1)
            unit = jnp.left_shift(1, lax.shift_right_logical(ids, rows.bit_length() - 1) * BITS)
            total = jnp.zeros((rows, LANES), jnp.int32)
            for p in range(bag):
                total = total + jnp.where(table_row == row[p : p + 1], unit[p : p + 1], 0)
            for j in range(FIELDS):
                field = lax.shift_right_logical(total, j * BITS) & ((1 << BITS) - 1)
                counts_ref[step, k, j * rows : (j + 1) * rows, cols] = field.astype(jnp.float32).astype(jnp.bfloat16)


def count(shard, ids, lengths, tables, vocab):
    feats, bag, batch = ids.shape
    chunk = 512
    return pl.pallas_call(
        count_kernel,
        grid_spec=pltpu.PrefetchScalarGridSpec(
            num_scalar_prefetch=1,
            grid=(batch // chunk,),
            in_specs=[
                pl.BlockSpec((feats, bag, chunk), lambda b, s: (0, 0, b)),
                pl.BlockSpec((feats, chunk), lambda b, s: (0, b)),
            ],
            out_specs=HELD,
        ),
        out_shape=pltpu.VMEM((batch // chunk, tables, vocab, chunk), jnp.bfloat16),
        compiler_params=params(14),
        cost_estimate=cost(tables * vocab * bag * batch, 4 * ids.size),
        name="count",
    )(shard, far(ids), far(lengths))


def pool_kernel(shard_ref, counts_ref, own_ref, other_ref, down_ref, up_ref, pooled_ref, first_ref, lead_ref, sems):
    part, width = own_ref.shape[1:]
    samples = pooled_ref.shape[2]
    chunk = counts_ref.shape[3]
    blocks = pooled_ref.shape[0] * samples // chunk
    k, step = pl.program_id(0), pl.program_id(1)
    fetches = [
        pltpu.make_async_copy(down_ref.at[: first_ref.shape[0]], first_ref, sems.at[0]),
        pltpu.make_async_copy(up_ref.at[:, : lead_ref.shape[1]], lead_ref, sems.at[1]),
    ]

    @pl.when((k == 0) & (step == 0))
    def _():
        for fetch in fetches:
            fetch.start()

    for c in range(blocks):
        total = jnp.zeros((width, chunk), jnp.float32)
        for place, table_ref in ((shard_ref[0], own_ref), (1 - shard_ref[0], other_ref)):
            rows = pl.ds(pl.multiple_of(place * part, part), part)
            total += lax.dot_general(
                table_ref[0], counts_ref[step * blocks + c, k, rows, :], (((0,), (0,)), ((), ())),
                preferred_element_type=jnp.float32,
            )
        owned = jnp.transpose(total.astype(jnp.bfloat16)).reshape(chunk // samples, samples, width)
        pooled_ref[c * (chunk // samples) : (c + 1) * (chunk // samples), 0] = owned

    @pl.when((k == pl.num_programs(0) - 1) & (step == pl.num_programs(1) - 1))
    def _():
        for fetch in fetches:
            fetch.wait()


def pool(shard, counts, tables, other, down, up, owners):
    chunks, pair, vocab, chunk = counts.shape
    batch = chunks * chunk
    part, width = tables.shape[1:]
    steps = 1
    return pl.pallas_call(
        pool_kernel,
        grid_spec=pltpu.PrefetchScalarGridSpec(
            num_scalar_prefetch=1,
            grid=(pair, steps),
            in_specs=[
                HELD,
                pl.BlockSpec((1, part, width), lambda k, b, s: (s[0] * pair + k, 0, 0)),
                pl.BlockSpec((1, part, width), lambda k, b, s: (k, 0, 0)),
                FAR,
                FAR,
            ],
            out_specs=[
                pl.BlockSpec((owners // steps, 1, batch // owners, width), lambda k, b, s: (b, k, 0, 0)),
                HELD,
                HELD,
            ],
            scratch_shapes=[pltpu.SemaphoreType.DMA((2,))],
        ),
        out_shape=[
            jax.ShapeDtypeStruct((owners, pair, batch // owners, width), jnp.bfloat16),
            pltpu.VMEM((down.shape[0] // STEPS * EARLY, down.shape[1]), down.dtype),
            pltpu.VMEM((up.shape[0], up.shape[1] // STEPS), up.dtype),
        ],
        compiler_params=params(14),
        cost_estimate=cost(2 * counts.size * width, 4 * counts.size),
        name="pool",
    )(shard, near(counts), tables, other, far(down), far(up))


def scatter_kernel(first, away, shard_ref, counts_ref, back_ref, grad_ref):
    owners, _, samples, width = back_ref.shape
    back = back_ref[:, 0].reshape(owners * samples, width)
    part = grad_ref.shape[1]
    half = 1 - shard_ref[0] if away else shard_ref[0]
    rows = pl.ds(pl.multiple_of(half * part, part), part)
    k = first + pl.program_id(0)
    counts = jnp.concatenate([counts_ref[c, k, rows, :] for c in range(counts_ref.shape[0])], axis=1)
    grad_ref[0] = jnp.dot(counts, back, preferred_element_type=jnp.float32).astype(jnp.bfloat16)


def scatter(shard, counts, back, shards, first, last, away):
    chunks, pair, vocab, chunk = counts.shape
    part = vocab // shards
    owners, _, samples, width = back.shape
    return pl.pallas_call(
        lambda *refs: scatter_kernel(first, away, *refs),
        grid_spec=pltpu.PrefetchScalarGridSpec(
            num_scalar_prefetch=1,
            grid=(last - first,),
            in_specs=[
                HELD,
                pl.BlockSpec((owners, 1, samples, width), lambda k, s: (0, first + k, 0, 0)),
            ],
            out_specs=pl.BlockSpec((1, part, width), lambda k, s: (k if away else s[0] * pair + first + k, 0, 0)),
        ),
        out_shape=jax.ShapeDtypeStruct((last - first if away else shards * pair, part, width), jnp.bfloat16),
        compiler_params=params(12),
        cost_estimate=cost(2 * counts.size // shards * width, 2 * counts.size // shards + 2 * back.size),
        name="scatter",
    )(shard, near(counts), back)


def row_of(x0_ref, groups):
    first = pl.program_id(0) * groups
    tables = x0_ref.shape[1]
    return jnp.concatenate([x0_ref[first + g, k] for g in range(groups) for k in range(tables)], axis=1)


def stream(steps, ahead, copy):
    step = pl.program_id(0)

    @pl.when(step == 0)
    def _():
        for i in range(1, min(ahead + 1, steps)):
            copy(i).start()

    @pl.when((step > 0) & (step + ahead < steps))
    def _():
        copy(step + ahead).start()

    @pl.when(step > 0)
    def _():
        copy(step).wait()


def in_parts(steps, work, first_ref, second_ref, lead_ref, piece_ref):
    step = pl.program_id(0)
    rows = first_ref.shape[0] // EARLY

    @pl.when(step == 0)
    def _():
        work(first_ref.at[:rows], lead_ref)

    @pl.when((step > 0) & (step < EARLY))
    def _():
        work(first_ref.at[pl.ds(pl.multiple_of(step * rows, rows), rows)], piece_ref)

    @pl.when(step >= EARLY)
    def _():
        work(second_ref.at[pl.ds(pl.multiple_of((step - EARLY) * rows, rows), rows)], piece_ref)


def project_kernel(
    steps, x0_ref, grad_ref, first_ref, lead_ref, down_ref, up_ref, sums_ref, second_ref, ring_ref, down_sems, sems
):
    samples = grad_ref.shape[0]
    width = grad_ref.shape[1] // steps
    step = pl.program_id(0)
    span = lambda i: pl.ds(pl.multiple_of(i * width, width), width)

    def copy(i):
        slot = lax.rem(i, AHEAD + 1)
        return pltpu.make_async_copy(up_ref.at[:, span(i)], ring_ref.at[slot], sems.at[slot])

    def second(i):
        return pltpu.make_async_copy(down_ref.at[span(EARLY + i), :], second_ref.at[span(i), :], down_sems.at[i])

    stream(steps, AHEAD, copy)

    @pl.when(step == 0)
    def _():
        for i in range(min(EARLY, steps - EARLY)):
            second(i).start()

    @pl.when((step > 0) & (step + EARLY - 1 < steps - EARLY))
    def _():
        second(step + EARLY - 1).start()

    @pl.when(step >= EARLY)
    def _():
        second(step - EARLY).wait()

    def work(down_part, up_part):
        x0 = row_of(x0_ref, x0_ref.shape[0] // steps)
        dgate = grad_ref[:, span(step)] * x0
        low = jnp.dot(x0, down_part[...], preferred_element_type=jnp.float32)
        dlow = lax.dot_general(
            dgate, up_part[...], (((1,), (1,)), ((), ())), preferred_element_type=jnp.float32
        )

        @pl.when(step == 0)
        def _():
            sums_ref[:samples] = low
            sums_ref[samples:] = dlow

        @pl.when(step > 0)
        def _():
            sums_ref[:samples] += low
            sums_ref[samples:] += dlow

    in_parts(steps, work, first_ref, second_ref, lead_ref, ring_ref.at[lax.rem(step, AHEAD + 1)])


def cross_kernel(
    steps, mine_ref, other_ref, x0_ref, first_ref, second_ref, lead_ref, up_ref, bias_ref, grad_ref, crossed_ref, back_ref, ring_ref, sems
):
    groups, tables, samples, cols = back_ref.shape
    width = groups * tables * cols
    step = pl.program_id(0)
    span = lambda i: pl.ds(pl.multiple_of(i * width, width), width)

    def copy(i):
        slot = lax.rem(i, 2)
        return pltpu.make_async_copy(up_ref.at[:, span(i)], ring_ref.at[slot], sems.at[slot])

    def work(down_part, up_part):
        sums = (mine_ref[...] + other_ref[...]).astype(jnp.bfloat16)
        spread = lax.dot_general(
            sums[samples:], down_part[...], (((1,), (1,)), ((), ())), preferred_element_type=jnp.float32
        )
        gate = jnp.dot(sums[:samples], up_part[...], preferred_element_type=jnp.float32)
        scale = gate + (bias_ref[...] + 1.0)
        x0 = row_of(x0_ref, groups).astype(jnp.float32)
        crossed_ref[...] = (x0 * scale).astype(jnp.bfloat16)
        upstream = grad_ref[:, span(step)].astype(jnp.float32)
        back = (upstream * scale + spread).astype(jnp.bfloat16)
        for g in range(groups):
            for k in range(tables):
                at = (g * tables + k) * cols
                back_ref[g, k] = back[:, at : at + cols]

    stream(steps, 1, copy)
    in_parts(steps, work, first_ref, second_ref, lead_ref, ring_ref.at[lax.rem(step, 2)])


def cross_layer(x0, first, lead, down, up, bias, grad):
    owners, tables, samples, cols = x0.shape
    rank = down.shape[1]
    steps = STEPS
    groups = owners // steps
    width = groups * tables * cols
    x0_spec = pl.BlockSpec((groups, tables, samples, cols), lambda i: (i, 0, 0, 0))
    row_spec = pl.BlockSpec((samples, width), lambda i: (0, i))
    sum_spec = pl.BlockSpec((2 * samples, rank), lambda i: (0, 0))
    ring = pltpu.VMEM((AHEAD + 1, rank, width), up.dtype)
    sems = pltpu.SemaphoreType.DMA((AHEAD + 1,))
    sums, second = pl.pallas_call(
        lambda *refs: project_kernel(steps, *refs),
        grid=(steps,),
        in_specs=[HELD, HELD, HELD, HELD, FAR, FAR],
        out_specs=[sum_spec, HELD],
        out_shape=[jax.ShapeDtypeStruct((2 * samples, rank), jnp.float32), pltpu.VMEM((down.shape[0] - first.shape[0], rank), down.dtype)],
        scratch_shapes=[ring, pltpu.SemaphoreType.DMA((steps - EARLY,)), sems],
        compiler_params=params(14),
        cost_estimate=cost(4 * x0.size * rank, 2 * up.size + 4 * x0.size),
        name="project",
    )(near(x0), near(grad), near(first), near(lead), far(down), far(up))
    other = lax.ppermute(sums, "row", [(0, 1), (1, 0)])
    return pl.pallas_call(
        lambda *refs: cross_kernel(steps, *refs),
        grid=(steps,),
        in_specs=[sum_spec, sum_spec, HELD, HELD, HELD, HELD, FAR, pl.BlockSpec((1, width), lambda i: (0, i)), HELD],
        out_specs=[row_spec, x0_spec],
        out_shape=[pltpu.HBM((samples, owners * tables * cols), jnp.bfloat16), pltpu.HBM(x0.shape, jnp.bfloat16)],
        scratch_shapes=[pltpu.VMEM((2, rank, width), up.dtype), pltpu.SemaphoreType.DMA((2,))],
        compiler_params=params(14),
        cost_estimate=cost(4 * x0.size * rank, 2 * up.size + 8 * x0.size),
        name="cross",
    )(sums, other, near(x0), near(first), near(second), near(lead), far(up), bias, near(grad))


def body(ids, lengths, tables, cross_down, cross_up, bias, grad_out):
    batch, feats, bag = ids.shape
    part, width = tables.shape[1:]
    shards = lax.axis_size("row")
    owners = lax.axis_size("table")
    pair = feats // shards
    shard = lax.axis_index("row").astype(jnp.int32)
    mine = shard.reshape(1)
    swap = [(0, 1), (1, 0)]
    sent = lax.dynamic_slice_in_dim(tables, (1 - shard) * pair, pair, 0)
    other = lax.ppermute(sent, "row", swap)
    ids, lengths = jnp.transpose(ids, (1, 2, 0)), jnp.transpose(lengths)
    counts = count(mine, ids, lengths, pair, shards * part)
    pooled, first, lead = pool(mine, counts, tables, other, cross_down, cross_up, owners)
    x0 = lax.all_to_all(pooled, "table", split_axis=0, concat_axis=0, tiled=True)
    crossed, x0_grad = cross_layer(x0, first, lead, cross_down, cross_up, bias.reshape(1, -1), grad_out)
    back = lax.all_to_all(x0_grad, "table", split_axis=0, concat_axis=0, tiled=True)
    cuts = [0, pair // 2, pair]
    incoming = []
    for first, last in zip(cuts, cuts[1:]):
        outgoing = scatter(mine, counts, back, shards, first, last, True)
        incoming.append(lax.ppermute(outgoing, "row", swap))
    table_grad = scatter(mine, counts, back, shards, 0, pair, False)
    incoming = jnp.concatenate(incoming, axis=0)
    table_grad = lax.dynamic_update_slice_in_dim(table_grad, incoming, (1 - shard) * pair, 0)
    return (crossed, table_grad)


def solution(mesh):
    in_specs = (
        P(None, "table", None),
        P(None, "table"),
        P("table", "row", None),
        P("row", None),
        P(None, "row"),
        P("row"),
        P("table", "row"),
    )
    out_specs = (P("table", "row"), P("table", "row", None))
    return jax.shard_map(body, mesh=mesh, in_specs=in_specs, out_specs=out_specs, check_vma=False)
```

```python
import jax
import jax.numpy as jnp
from jax import lax
from jax.experimental import pallas as pl
from jax.experimental.pallas import tpu as pltpu
from jax.sharding import PartitionSpec as P

FIELDS = 8
BITS = 4
LANES = 128
MIB = 1 << 20
AHEAD = 2
STEPS = 8
EARLY = 2
HELD = pl.BlockSpec(memory_space=pltpu.VMEM)
FAR = pl.BlockSpec(memory_space=pl.ANY)


def near(x):
    return pltpu.with_memory_space_constraint(x, pltpu.VMEM)


def far(x):
    return pltpu.with_memory_space_constraint(x, pltpu.HBM)


def params(mib):
    return pltpu.CompilerParams(vmem_limit_bytes=mib * MIB)


def cost(flops, moved):
    return pl.CostEstimate(flops=flops, bytes_accessed=moved, transcendentals=0)


def count_kernel(shard_ref, ids_ref, lengths_ref, counts_ref):
    tables, vocab = counts_ref.shape[1:3]
    bag, batch = ids_ref.shape[1:]
    rows = vocab // FIELDS
    feat = shard_ref[0] * tables
    step = pl.program_id(0)
    slot = lax.broadcasted_iota(jnp.int32, (bag, LANES), 0)
    table_row = lax.broadcasted_iota(jnp.int32, (rows, LANES), 0)
    for k in range(tables):
        for start in range(0, batch, LANES):
            cols = pl.ds(start, LANES)
            ids = ids_ref[feat + k, :, cols]
            length = lengths_ref[k : k + 1, cols]
            for other in range(1, lengths_ref.shape[0] // tables):
                at = other * tables + k
                length = jnp.where(shard_ref[0] == other, lengths_ref[at : at + 1, cols], length)
            row = jnp.where(slot < length, ids & (rows - 1), -1)
            unit = jnp.left_shift(1, lax.shift_right_logical(ids, rows.bit_length() - 1) * BITS)
            total = jnp.zeros((rows, LANES), jnp.int32)
            for p in range(bag):
                total = total + jnp.where(table_row == row[p : p + 1], unit[p : p + 1], 0)
            for j in range(FIELDS):
                field = lax.shift_right_logical(total, j * BITS) & ((1 << BITS) - 1)
                counts_ref[step, k, j * rows : (j + 1) * rows, cols] = field.astype(jnp.float32).astype(jnp.bfloat16)


def count(shard, ids, lengths, tables, vocab):
    feats, bag, batch = ids.shape
    chunk = 512
    return pl.pallas_call(
        count_kernel,
        grid_spec=pltpu.PrefetchScalarGridSpec(
            num_scalar_prefetch=1,
            grid=(batch // chunk,),
            in_specs=[
                pl.BlockSpec((feats, bag, chunk), lambda b, s: (0, 0, b)),
                pl.BlockSpec((feats, chunk), lambda b, s: (0, b)),
            ],
            out_specs=HELD,
        ),
        out_shape=pltpu.VMEM((batch // chunk, tables, vocab, chunk), jnp.bfloat16),
        compiler_params=params(14),
        cost_estimate=cost(tables * vocab * bag * batch, 4 * ids.size),
        name="count",
    )(shard, far(ids), far(lengths))


def pool_kernel(shard_ref, counts_ref, own_ref, other_ref, down_ref, up_ref, pooled_ref, first_ref, lead_ref, sems):
    part, width = own_ref.shape[1:]
    samples = pooled_ref.shape[2]
    chunk = counts_ref.shape[3]
    blocks = pooled_ref.shape[0] * samples // chunk
    k, step = pl.program_id(0), pl.program_id(1)
    fetches = [
        pltpu.make_async_copy(down_ref.at[: first_ref.shape[0]], first_ref, sems.at[0]),
        pltpu.make_async_copy(up_ref.at[:, : lead_ref.shape[1]], lead_ref, sems.at[1]),
    ]

    @pl.when((k == 0) & (step == 0))
    def _():
        for fetch in fetches:
            fetch.start()

    for c in range(blocks):
        total = jnp.zeros((width, chunk), jnp.float32)
        for place, table_ref in ((shard_ref[0], own_ref), (1 - shard_ref[0], other_ref)):
            rows = pl.ds(pl.multiple_of(place * part, part), part)
            total += lax.dot_general(
                table_ref[0], counts_ref[step * blocks + c, k, rows, :], (((0,), (0,)), ((), ())),
                preferred_element_type=jnp.float32,
            )
        owned = jnp.transpose(total.astype(jnp.bfloat16)).reshape(chunk // samples, samples, width)
        pooled_ref[c * (chunk // samples) : (c + 1) * (chunk // samples), 0] = owned

    @pl.when((k == pl.num_programs(0) - 1) & (step == pl.num_programs(1) - 1))
    def _():
        for fetch in fetches:
            fetch.wait()


def pool(shard, counts, tables, other, down, up, owners):
    chunks, pair, vocab, chunk = counts.shape
    batch = chunks * chunk
    part, width = tables.shape[1:]
    steps = 1
    return pl.pallas_call(
        pool_kernel,
        grid_spec=pltpu.PrefetchScalarGridSpec(
            num_scalar_prefetch=1,
            grid=(pair, steps),
            in_specs=[
                HELD,
                pl.BlockSpec((1, part, width), lambda k, b, s: (s[0] * pair + k, 0, 0)),
                pl.BlockSpec((1, part, width), lambda k, b, s: (k, 0, 0)),
                FAR,
                FAR,
            ],
            out_specs=[
                pl.BlockSpec((owners // steps, 1, batch // owners, width), lambda k, b, s: (b, k, 0, 0)),
                HELD,
                HELD,
            ],
            scratch_shapes=[pltpu.SemaphoreType.DMA((2,))],
        ),
        out_shape=[
            jax.ShapeDtypeStruct((owners, pair, batch // owners, width), jnp.bfloat16),
            pltpu.VMEM((down.shape[0] // STEPS * EARLY, down.shape[1]), down.dtype),
            pltpu.VMEM((up.shape[0], up.shape[1] // STEPS), up.dtype),
        ],
        compiler_params=params(14),
        cost_estimate=cost(2 * counts.size * width, 4 * counts.size),
        name="pool",
    )(shard, near(counts), tables, other, far(down), far(up))


def scatter_kernel(first, away, shard_ref, counts_ref, back_ref, grad_ref):
    owners, together, samples, width = back_ref.shape
    part = grad_ref.shape[1]
    half = 1 - shard_ref[0] if away else shard_ref[0]
    rows = pl.ds(pl.multiple_of(half * part, part), part)
    for t in range(together):
        k = first + pl.program_id(0) * together + t
        back = back_ref[:, t].reshape(owners * samples, width)
        counts = jnp.concatenate([counts_ref[c, k, rows, :] for c in range(counts_ref.shape[0])], axis=1)
        grad_ref[t] = jnp.dot(counts, back, preferred_element_type=jnp.float32).astype(jnp.bfloat16)


def scatter(shard, counts, back, shards, first, last, away):
    chunks, pair, vocab, chunk = counts.shape
    part = vocab // shards
    owners, _, samples, width = back.shape
    together = pair // 2
    return pl.pallas_call(
        lambda *refs: scatter_kernel(first, away, *refs),
        grid_spec=pltpu.PrefetchScalarGridSpec(
            num_scalar_prefetch=1,
            grid=((last - first) // together,),
            in_specs=[
                HELD,
                pl.BlockSpec((owners, together, samples, width), lambda k, s: (0, first // together + k, 0, 0)),
            ],
            out_specs=pl.BlockSpec(
                (together, part, width),
                lambda k, s: (k if away else (s[0] * pair + first) // together + k, 0, 0),
            ),
        ),
        out_shape=jax.ShapeDtypeStruct((last - first if away else shards * pair, part, width), jnp.bfloat16),
        compiler_params=params(12),
        cost_estimate=cost(2 * counts.size // shards * width, 2 * counts.size // shards + 2 * back.size),
        name="scatter",
    )(shard, near(counts), back)


def row_of(x0_ref, groups):
    first = pl.program_id(0) * groups
    tables = x0_ref.shape[1]
    return jnp.concatenate([x0_ref[first + g, k] for g in range(groups) for k in range(tables)], axis=1)


def stream(steps, ahead, copy):
    step = pl.program_id(0)

    @pl.when(step == 0)
    def _():
        for i in range(1, min(ahead + 1, steps)):
            copy(i).start()

    @pl.when((step > 0) & (step + ahead < steps))
    def _():
        copy(step + ahead).start()

    @pl.when(step > 0)
    def _():
        copy(step).wait()


def in_parts(steps, work, first_ref, second_ref, lead_ref, piece_ref):
    step = pl.program_id(0)
    rows = first_ref.shape[0] // EARLY

    @pl.when(step == 0)
    def _():
        work(first_ref.at[:rows], lead_ref)

    @pl.when((step > 0) & (step < EARLY))
    def _():
        work(first_ref.at[pl.ds(pl.multiple_of(step * rows, rows), rows)], piece_ref)

    @pl.when(step >= EARLY)
    def _():
        work(second_ref.at[pl.ds(pl.multiple_of((step - EARLY) * rows, rows), rows)], piece_ref)


def project_kernel(
    steps, x0_ref, grad_ref, first_ref, lead_ref, down_ref, up_ref, sums_ref, second_ref, ring_ref, down_sems, sems
):
    samples = grad_ref.shape[0]
    width = grad_ref.shape[1] // steps
    step = pl.program_id(0)
    span = lambda i: pl.ds(pl.multiple_of(i * width, width), width)

    def copy(i):
        slot = lax.rem(i, AHEAD + 1)
        return pltpu.make_async_copy(up_ref.at[:, span(i)], ring_ref.at[slot], sems.at[slot])

    def second(i):
        return pltpu.make_async_copy(down_ref.at[span(EARLY + i), :], second_ref.at[span(i), :], down_sems.at[i])

    stream(steps, AHEAD, copy)

    @pl.when(step == 0)
    def _():
        for i in range(min(EARLY, steps - EARLY)):
            second(i).start()

    @pl.when((step > 0) & (step + EARLY - 1 < steps - EARLY))
    def _():
        second(step + EARLY - 1).start()

    @pl.when(step >= EARLY)
    def _():
        second(step - EARLY).wait()

    def work(down_part, up_part):
        x0 = row_of(x0_ref, x0_ref.shape[0] // steps)
        dgate = grad_ref[:, span(step)] * x0
        low = jnp.dot(x0, down_part[...], preferred_element_type=jnp.float32)
        dlow = lax.dot_general(
            dgate, up_part[...], (((1,), (1,)), ((), ())), preferred_element_type=jnp.float32
        )

        @pl.when(step == 0)
        def _():
            sums_ref[:samples] = low
            sums_ref[samples:] = dlow

        @pl.when(step > 0)
        def _():
            sums_ref[:samples] += low
            sums_ref[samples:] += dlow

    in_parts(steps, work, first_ref, second_ref, lead_ref, ring_ref.at[lax.rem(step, AHEAD + 1)])


def cross_kernel(
    steps, mine_ref, other_ref, x0_ref, first_ref, second_ref, lead_ref, up_ref, bias_ref, grad_ref, crossed_ref, back_ref, ring_ref, sems
):
    groups, tables, samples, cols = back_ref.shape
    width = groups * tables * cols
    step = pl.program_id(0)
    span = lambda i: pl.ds(pl.multiple_of(i * width, width), width)

    def copy(i):
        slot = lax.rem(i, 2)
        return pltpu.make_async_copy(up_ref.at[:, span(i)], ring_ref.at[slot], sems.at[slot])

    def work(down_part, up_part):
        sums = (mine_ref[...] + other_ref[...]).astype(jnp.bfloat16)
        spread = lax.dot_general(
            sums[samples:], down_part[...], (((1,), (1,)), ((), ())), preferred_element_type=jnp.float32
        )
        gate = jnp.dot(sums[:samples], up_part[...], preferred_element_type=jnp.float32)
        scale = gate + (bias_ref[...] + 1.0)
        x0 = row_of(x0_ref, groups).astype(jnp.float32)
        crossed_ref[...] = (x0 * scale).astype(jnp.bfloat16)
        upstream = grad_ref[:, span(step)].astype(jnp.float32)
        back = (upstream * scale + spread).astype(jnp.bfloat16)
        for g in range(groups):
            for k in range(tables):
                at = (g * tables + k) * cols
                back_ref[g, k] = back[:, at : at + cols]

    stream(steps, 1, copy)
    in_parts(steps, work, first_ref, second_ref, lead_ref, ring_ref.at[lax.rem(step, 2)])


def cross_layer(x0, first, lead, down, up, bias, grad):
    owners, tables, samples, cols = x0.shape
    rank = down.shape[1]
    steps = STEPS
    groups = owners // steps
    width = groups * tables * cols
    x0_spec = pl.BlockSpec((groups, tables, samples, cols), lambda i: (i, 0, 0, 0))
    row_spec = pl.BlockSpec((samples, width), lambda i: (0, i))
    sum_spec = pl.BlockSpec((2 * samples, rank), lambda i: (0, 0))
    ring = pltpu.VMEM((AHEAD + 1, rank, width), up.dtype)
    sems = pltpu.SemaphoreType.DMA((AHEAD + 1,))
    sums, second = pl.pallas_call(
        lambda *refs: project_kernel(steps, *refs),
        grid=(steps,),
        in_specs=[HELD, HELD, HELD, HELD, FAR, FAR],
        out_specs=[sum_spec, HELD],
        out_shape=[jax.ShapeDtypeStruct((2 * samples, rank), jnp.float32), pltpu.VMEM((down.shape[0] - first.shape[0], rank), down.dtype)],
        scratch_shapes=[ring, pltpu.SemaphoreType.DMA((steps - EARLY,)), sems],
        compiler_params=params(14),
        cost_estimate=cost(4 * x0.size * rank, 2 * up.size + 4 * x0.size),
        name="project",
    )(near(x0), near(grad), near(first), near(lead), far(down), far(up))
    other = lax.ppermute(sums, "row", [(0, 1), (1, 0)])
    return pl.pallas_call(
        lambda *refs: cross_kernel(steps, *refs),
        grid=(steps,),
        in_specs=[sum_spec, sum_spec, HELD, HELD, HELD, HELD, FAR, pl.BlockSpec((1, width), lambda i: (0, i)), HELD],
        out_specs=[row_spec, x0_spec],
        out_shape=[pltpu.HBM((samples, owners * tables * cols), jnp.bfloat16), pltpu.HBM(x0.shape, jnp.bfloat16)],
        scratch_shapes=[pltpu.VMEM((2, rank, width), up.dtype), pltpu.SemaphoreType.DMA((2,))],
        compiler_params=params(14),
        cost_estimate=cost(4 * x0.size * rank, 2 * up.size + 8 * x0.size),
        name="cross",
    )(sums, other, near(x0), near(first), near(second), near(lead), far(up), bias, near(grad))


def body(ids, lengths, tables, cross_down, cross_up, bias, grad_out):
    batch, feats, bag = ids.shape
    part, width = tables.shape[1:]
    shards = lax.axis_size("row")
    owners = lax.axis_size("table")
    pair = feats // shards
    shard = lax.axis_index("row").astype(jnp.int32)
    mine = shard.reshape(1)
    swap = [(0, 1), (1, 0)]
    sent = lax.dynamic_slice_in_dim(tables, (1 - shard) * pair, pair, 0)
    other = lax.ppermute(sent, "row", swap)
    ids, lengths = jnp.transpose(ids, (1, 2, 0)), jnp.transpose(lengths)
    counts = count(mine, ids, lengths, pair, shards * part)
    pooled, first, lead = pool(mine, counts, tables, other, cross_down, cross_up, owners)
    x0 = lax.all_to_all(pooled, "table", split_axis=0, concat_axis=0, tiled=True)
    crossed, x0_grad = cross_layer(x0, first, lead, cross_down, cross_up, bias.reshape(1, -1), grad_out)
    back = lax.all_to_all(x0_grad, "table", split_axis=0, concat_axis=0, tiled=True)
    cuts = [0, pair // 2, pair]
    incoming = []
    for first, last in zip(cuts, cuts[1:]):
        outgoing = scatter(mine, counts, back, shards, first, last, True)
        incoming.append(lax.ppermute(outgoing, "row", swap))
    table_grad = scatter(mine, counts, back, shards, 0, pair, False)
    incoming = jnp.concatenate(incoming, axis=0)
    table_grad = lax.dynamic_update_slice_in_dim(table_grad, incoming, (1 - shard) * pair, 0)
    return (crossed, table_grad)


def solution(mesh):
    in_specs = (
        P(None, "table", None),
        P(None, "table"),
        P("table", "row", None),
        P("row", None),
        P(None, "row"),
        P("row"),
        P("table", "row"),
    )
    out_specs = (P("table", "row"), P("table", "row", None))
    return jax.shard_map(body, mesh=mesh, in_specs=in_specs, out_specs=out_specs, check_vma=False)
```
